256 devices in a mesh: grp: 64 (over x, z, core), slab: 4 (over y).
Axes of the slice: x: 4, y: 4, z: 8, core: 2. Of those that a mesh axis runs over, the one named last changes fastest.
Arguments:
- support: bfloat16 [1024, 32, 32, 128], P('grp', None, 'slab'), may hold values from -6 to 6
- corners: int32 [1024], P('grp'), may hold values from 0 to 2047, as said below
- occupation: bfloat16 [1024], P('grp'), may hold values from 0.019897461 to 0.099609375
- potential: float32 [2048, 32, 128], P('grp', 'slab'), may hold values from -4 to 4
Outputs:
- applied: bfloat16 [1024, 32, 32, 128], P('grp', None, 'slab')
- density: float32 [2048, 32, 128], P('grp', 'slab')
The draws below stay inside these ranges and needn't reach their ends.
Inputs may be any that keep to these rules, and one draw needn't show every extreme that they name: corners[k] starts a region of 32 consecutive y planes counted modulo 2048. All regions of one group (the 16 consecutive functions held by one grp index) start at the same offset modulo 32. Of one group's region planes at most 32 lie in one block of planes b*32 to b*32 + 31, and in every draw some block receives exactly 32 from every group.
All inputs are finite; a program needn't handle non-finite values.
Results may differ from the reference program's by a relative error of at most 0.0045.
Values may be sent and summed in bfloat16 or wider, within the bound.
A program may use at most 192 MiB of HBM per device.

```python
import math
import jax
import jax.numpy as jnp
from jax import lax

CY = 32
SF_DEV = 16
NZ = 128
NY = 2048
NX = 32
SFS = 1024
N_GRP = 64


def draw_corners(key, part):
    key = jax.random.fold_in(key, 11)
    key_hot, key_shift, key_perm = jax.random.split(key, 3)
    hottest = jax.random.randint(key_hot, (), 0, N_GRP)
    shifts = jax.random.randint(key_shift, (N_GRP,), 0, CY)
    perm_keys = jax.random.split(key_perm, N_GRP)
    perms = jax.vmap(lambda single: jax.random.permutation(single, N_GRP))(perm_keys)
    owners = jnp.arange(N_GRP, dtype=jnp.int32)[None, :]
    scores = jnp.where(owners == hottest, -2, jnp.where(owners == (hottest - 1) % N_GRP, -1, perms))
    order = jnp.argsort(scores, axis=1, stable=True)
    picks = jnp.arange(SF_DEV, dtype=jnp.int32) % N_GRP
    bases = order[:, picks]
    corners = bases * CY + shifts[:, None]
    return corners.reshape(-1).astype(jnp.int32)


def block_scale(key, extent, shards, least, top_value):
    factor_of, own = 1.0, jax.random.fold_in(key, 6)
    for axis_at, shards_of in shards:
        draws = jnp.exp(jax.random.uniform(jax.random.fold_in(own, axis_at), (shards_of,), jnp.float32, least / len(shards), top_value / len(shards)))
        factor_of = factor_of * jnp.repeat(draws, extent[axis_at] // shards_of).reshape([-1 if axis == axis_at else 1 for axis in range(len(extent))])
    return factor_of


def normal_values(rng, extent, width, limit, cuts=(), kind=jnp.bfloat16):
    array = width * jax.random.normal(rng, extent, jnp.float32)
    if cuts:
        array = array * block_scale(rng, extent, cuts, -0.22, 0.18)
    return jnp.clip(array, -limit, limit).astype(kind)


def setup_inputs(seed: int = 0) -> dict:
    streams_of = jax.random.split(jax.random.key(seed), 5)
    support = normal_values(streams_of[0], (SFS, CY, NX, NZ), 1.0, 6.0, ((0, 64), (2, 4)))
    corners = draw_corners(jax.random.fold_in(streams_of[4], 71), 0)
    occupation = jnp.clip(jnp.exp(math.log(0.099609375) - 1.61066415 * jax.random.uniform(streams_of[2], (SFS,), jnp.float32) ** block_scale(streams_of[2], (SFS,), ((0, 64),), -0.2, 0.2)), 0.019897461, 0.099609375).astype(jnp.bfloat16)
    potential = normal_values(streams_of[3], (NY, NX, NZ), 1.0, 4.0, ((0, 64), (1, 4)), jnp.float32)
    return {"support": support, "corners": corners, "occupation": occupation, "potential": potential}


kinetic_taps = [2.0 * (-1.0) ** (index + 2) / float((index + 1) * (index + 1)) for index in range(8)]
center_tap = -math.pi * math.pi / 3.0


def laplace(values):
    total = 3.0 * center_tap * values
    padded = jnp.pad(values, ((0, 0), (8, 8), (0, 0), (0, 0)))
    planes = values.shape[1]
    for offset in range(1, 9):
        weight = kinetic_taps[offset - 1]
        along_y = padded[:, 8 + offset:8 + offset + planes] + padded[:, 8 - offset:8 - offset + planes]
        along_x = jnp.roll(values, offset, 2) + jnp.roll(values, -offset, 2)
        along_z = jnp.roll(values, offset, 3) + jnp.roll(values, -offset, 3)
        total = total + weight * (along_y + along_x + along_z)
    return total


def reference(support, corners, occupation, potential):
    def one_group(density, block):
        funcs, starts, weights = block
        plane = (starts[:, None] + jnp.arange(CY, dtype=jnp.int32)[None, :]) % NY
        values = funcs.astype(jnp.float32)
        laplace_term = laplace(values)
        potential_term = (potential[plane] * values).astype(jnp.bfloat16)
        potential_term = lax.optimization_barrier(potential_term)
        applied = (-0.5 * laplace_term + potential_term.astype(jnp.float32)).astype(jnp.bfloat16)
        terms = weights.astype(jnp.float32)[:, None, None, None] * values * values
        density = density.at[plane.reshape(-1)].add(terms.reshape(-1, NX, NZ))
        return density, applied

    start = jnp.zeros((NY, NX, NZ), jnp.float32)
    blocks = (support.reshape(N_GRP, SF_DEV, CY, NX, NZ), corners.reshape(N_GRP, SF_DEV),
              occupation.reshape(N_GRP, SF_DEV))
    density, applied = lax.scan(one_group, start, blocks)
    return applied.reshape(SFS, CY, NX, NZ), density
```

```python
import functools
import math

import jax
import jax.numpy as jnp
import numpy as np
from jax import lax
from jax.experimental import pallas as pl
from jax.experimental.pallas import tpu as pltpu
from jax.sharding import PartitionSpec as P

MESH = pl.DeviceIdType.MESH
FUNCS, ROWS, LANES = 16, 256, 128
NXC, NZC = 4, 8
PAIRS = FUNCS // 2
TILE = 16
PLANES, TILES = ROWS // 8, ROWS // TILE
RA = 160
RB = ROWS - RA
HA, HB = RA // 2, RB // 2

kinetic_taps = [
    2.0 * (-1.0) ** (index + 2) / float((index + 1) * (index + 1)) for index in range(8)
]
center_tap = -math.pi * math.pi / 3.0


def split_bf16(matrix):
    high = matrix.astype(jnp.bfloat16)
    low = (matrix - high.astype(np.float64)).astype(jnp.bfloat16)
    return high, low


def stencil_matrices():
    along_y, along_x = np.zeros((32, 32)), np.zeros((8, 8))
    left, right, along_z = np.zeros((8, 8)), np.zeros((8, 8)), np.zeros((LANES, LANES))
    for offset in range(1, 9):
        weight = kinetic_taps[offset - 1]
        along_y += weight * (np.eye(32, k=offset) + np.eye(32, k=-offset))
        along_x += weight * (np.eye(8, k=offset) + np.eye(8, k=-offset))
        left += weight * np.eye(8, k=8 - offset)
        right += weight * np.eye(8, k=offset - 8)
        along_z += weight * (
            np.roll(np.eye(LANES), offset, 1) + np.roll(np.eye(LANES), -offset, 1)
        )
    own = (
        np.kron(along_y, np.eye(8))
        + np.kron(np.eye(32), along_x)
        + 3.0 * center_tap * np.eye(ROWS)
    )
    rows = np.concatenate(
        [own, np.kron(np.eye(32), left), np.kron(np.eye(32), right)], axis=1
    )
    rows_high, rows_low = split_bf16(-0.5 * rows)
    z_high, z_low = split_bf16(-0.5 * along_z)
    return np.stack([rows_high, rows_low]), np.concatenate([z_high, z_low], axis=0)


def kernel(
    corners, occupation, support, potential, row_weights_in, z_weights_in,
    applied, density,
    own, left, right, out, pot_in, dens, row_weights, z_weights,
    gathered, terms, table, part_out, part_in, sums,
    xa1, xa2, za1, za, zb1, zb, xb1, xb2,
    load_sem, out_sem, send_sem, recv_sem,
):
    f32, bf16 = jnp.float32, jnp.bfloat16
    group, slab = lax.axis_index("grp"), lax.axis_index("slab")
    x, z, core = group // 16, (group // 2) % 8, group % 2

    def chip(dx, dz):
        return ((((x + dx) % NXC) * NZC + (z + dz) % NZC) * 2 + core, slab)

    partner = (group + 1 - 2 * core, slab)
    x_next, x_prev = chip(1, 0), chip(NXC - 1, 0)
    z_next, z_prev = chip(0, 1), chip(0, NZC - 1)
    y_next, y_prev = (group, (slab + 1) % 4), (group, (slab + 3) % 4)
    along_x, along_z, along_y = (x_next, x_prev), (z_next, z_prev), (y_next, y_prev)

    loads = {}
    for index, (name, src, dst) in enumerate([
        ("potential", potential, pot_in),
        ("support", support, own),
        ("rows", row_weights_in, row_weights),
        ("z", z_weights_in, z_weights),
    ]):
        loads[name] = pltpu.make_async_copy(src, dst, load_sem.at[index])
        loads[name].start()

    sent = {}

    def send(name, src, dst, device):
        index = len(sent)
        copy = pltpu.make_async_remote_copy(
            src_ref=src, dst_ref=dst,
            send_sem=send_sem.at[index], recv_sem=recv_sem.at[index],
            device_id=device, device_id_type=MESH,
        )
        copy.start()
        sent[name] = copy

    def arrived(*name):
        sent[name].wait_recv()

    barrier = pltpu.get_barrier_semaphore()
    neighbours = (*along_x, *along_z, *along_y, partner)
    for device in neighbours:
        pl.semaphore_signal(barrier, inc=1, device_id=device, device_id_type=MESH)
    pl.semaphore_wait(barrier, len(neighbours))

    def slot(dx, dz, start, size):
        tiles = pl.ds(start // TILE, size // TILE)
        return gathered.at[(x + dx) % NXC, (z + dz) % NZC, core, tiles]

    def column(dz, start, size):
        tiles = pl.ds(start // TILE, size // TILE)
        return gathered.at[pl.ds(0, NXC), (z + dz) % NZC, core, tiles]

    def a_z(step):
        for way in range(2):
            dz = (NZC - (step - 1)) % NZC if way == 0 else step - 1
            where = slot(0, dz, 0, RA) if step < 4 else slot(0, dz, way * HA, HA)
            send(("az", step, way), where, where, along_z[way])

    def a_x1(dz):
        for way in range(2):
            where = slot(0, dz, 0, RA)
            send(("ax1", dz, way), where, where, along_x[way])

    def a_x2(dz):
        for way in range(2):
            arrived("ax1", dz, way)
            where = slot(3 if way == 0 else 1, dz, way * HA, HA)
            send(("ax2", dz, way), where, where, along_x[way])

    def a_partner(dz):
        for way in range(2):
            arrived("ax2", dz, way)
        where = column(dz, 0, RA)
        send(("ap", dz), where, where, partner)

    def b_x1():
        for way in range(2):
            where = slot(0, 0, RA, RB)
            send(("bx1", way), where, where, along_x[way])

    def b_x2():
        for way in range(2):
            arrived("bx1", way)
            where = slot(3 if way == 0 else 1, 0, RA + way * HB, HB)
            send(("bx2", way), where, where, along_x[way])

    def b_z(step):
        for way in range(2):
            dz = (NZC - (step - 1)) % NZC if way == 0 else step - 1
            where = column(dz, RA, RB) if step < 4 else column(dz, RA + way * HB, HB)
            send(("bz", step, way), where, where, along_z[way])

    def b_partner(dz):
        where = column(dz, RA, RB)
        send(("bp", dz), where, where, partner)

    def gather_step(step):
        if step == 0:
            a_z(1)
            a_x1(0)
            b_x1()
            return
        if step <= 4:
            for way in range(2):
                arrived("az", step, way)
            if step < 4:
                a_z(step + 1)
                a_x1(NZC - step)
                a_x1(step)
            else:
                a_x1(4)
        if step == 1:
            a_x2(0)
            b_x2()
        elif step <= 4:
            a_x2(NZC - step + 1)
            a_x2(step - 1)
        elif step == 5:
            a_x2(4)
        if step == 2:
            for way in range(2):
                arrived("bx2", way)
            b_z(1)
            b_partner(0)
            a_partner(0)
        elif step >= 3:
            for way in range(2):
                arrived("bz", step - 2, way)
            if step < 6:
                b_z(step - 1)
                b_partner(NZC - (step - 2))
                b_partner(step - 2)
                a_partner(NZC - (step - 2))
                a_partner(step - 2)
            else:
                b_partner(4)
                a_partner(4)

    def gather_end():
        for dz in range(NZC):
            arrived("ap", dz)
            arrived("bp", dz)
        gathered[4, 0, 0] = gathered[0, 0, 0]

    def build(target, dz, owner, added=None):
        shift = corners[0] % PLANES

        def one(dx, carry):
            block = ((x + dx) % NXC) * 16 + ((z + dz) % NZC) * 2 + owner
            after = table[block] - shift
            before = table[(block + 63) % 64] + PLANES - shift
            for at in range(0, PLANES, 2):
                planes = [
                    terms[plane + jnp.where(plane >= shift, after, before)]
                    for plane in (at, at + 1)
                ]
                value = jnp.concatenate(planes, axis=0)
                rows = pl.ds(at * 8, TILE)
                if added is not None:
                    value = value + added[dz, dx, rows, :].astype(f32)
                target[dz, dx, rows, :] = value.astype(bf16)
            return carry

        lax.fori_loop(0, NXC, one, 0)

    def build_partner(dz):
        build(part_out, dz, 1 - core)
        send(("part", dz), part_out.at[dz], part_in.at[dz], partner)

    def build_own(dz):
        arrived("part", dz)
        build(sums, dz, core, part_in)

    def add(where, start, size, *others):
        total = where[pl.ds(start, size), :].astype(f32)
        for other in others:
            total = total + other[...].astype(f32)
        where[pl.ds(start, size), :] = total.astype(bf16)

    def add4(dz, start, size, *others):
        for dx in range(NXC):
            add(sums.at[dz, dx], start, size, *[other.at[dx] for other in others])

    def ra_x1(dz):
        for way in range(2):
            send(("rax1", dz, way), sums.at[dz, 2, pl.ds(way * HA, HA)], xa1.at[dz, way], along_x[way])

    def ra_x2(dz):
        for way in range(2):
            dx = 1 if way == 0 else 3
            arrived("rax1", dz, way)
            add(sums.at[dz, dx], way * HA, HA, xa1.at[dz, way])
            send(("rax2", dz, way), sums.at[dz, dx, pl.ds(0, RA)], xa2.at[dz, way], along_x[way])

    def ra_x3(dz):
        for way in range(2):
            arrived("rax2", dz, way)
        add(sums.at[dz, 0], 0, RA, xa2.at[dz, 0], xa2.at[dz, 1])

    def ra_z(step):
        for way in range(2):
            if step == 1:
                send(("raz", 1, way), sums.at[4, 0, pl.ds(way * HA, HA)], za1.at[way], along_z[way])
                continue
            dz = 5 - step if way == 0 else 3 + step
            arrived("raz", step - 1, way)
            if step == 2:
                add(sums.at[dz, 0], way * HA, HA, za1.at[way])
            else:
                add(sums.at[dz, 0], 0, RA, za.at[step - 3, way])
            send(("raz", step, way), sums.at[dz, 0, pl.ds(0, RA)], za.at[step - 2, way], along_z[way])

    def rb_z(step):
        for way in range(2):
            if step == 1:
                send(("rbz", 1, way), sums.at[4, :, pl.ds(RA + way * HB, HB)], zb1.at[way], along_z[way])
                continue
            dz = 5 - step if way == 0 else 3 + step
            arrived("rbz", step - 1, way)
            if step == 2:
                add4(dz, RA + way * HB, HB, zb1.at[way])
            else:
                add4(dz, RA, RB, zb.at[step - 3, way])
            send(("rbz", step, way), sums.at[dz, :, pl.ds(RA, RB)], zb.at[step - 2, way], along_z[way])

    def rb_x1():
        for way in range(2):
            arrived("rbz", 4, way)
        add4(0, RA, RB, zb.at[2, 0], zb.at[2, 1])
        for way in range(2):
            send(("rbx1", way), sums.at[0, 2, pl.ds(RA + way * HB, HB)], xb1.at[way], along_x[way])

    def rb_x2():
        for way in range(2):
            dx = 1 if way == 0 else 3
            arrived("rbx1", way)
            add(sums.at[0, dx], RA + way * HB, HB, xb1.at[way])
            send(("rbx2", way), sums.at[0, dx, pl.ds(RA, RB)], xb2.at[way], along_x[way])

    levels = [(4,), (3, 5), (2, 6), (1, 7), (0,)]

    def scatter_step(step):
        if step <= 3:
            rb_z(step + 1)
        elif step == 4:
            rb_x1()
        elif step == 5:
            rb_x2()
        if step >= 2:
            for dz in levels[step - 2]:
                ra_x3(dz)
            if step < 6:
                ra_z(step - 1)
        if 1 <= step <= 5:
            for dz in levels[step - 1]:
                ra_x2(dz)
        if step <= 4:
            for dz in levels[step]:
                ra_x1(dz)

    def scatter_end():
        for way in range(2):
            arrived("raz", 4, way)
        dens[pl.ds(0, RA), :] = (
            sums[0, 0, pl.ds(0, RA), :].astype(f32)
            + za[2, 0].astype(f32) + za[2, 1].astype(f32)
        )
        for way in range(2):
            arrived("rbx2", way)
        dens[pl.ds(RA, RB), :] = (
            sums[0, 0, pl.ds(RA, RB), :].astype(f32)
            + xb2[0].astype(f32) + xb2[1].astype(f32)
        )
        copy = pltpu.make_async_copy(dens, density, out_sem.at[PAIRS])
        copy.start()
        loads["density"] = copy

    def apply(pair):
        arrived("halo", pair, 0)
        arrived("halo", pair, 1)
        first = 2 * pair
        both = [
            jnp.concatenate([ref[first], ref[first + 1]], axis=1) for ref in (own, left, right)
        ]
        cells = jnp.concatenate(both, axis=0)
        total = jnp.dot(row_weights[0], cells, preferred_element_type=f32)
        total = total + jnp.dot(row_weights[1], cells, preferred_element_type=f32)
        flat = gathered.reshape(5 * NZC * 2 * TILES, TILE, LANES)
        for index in range(2):
            values = own[first + index]
            twice = jnp.concatenate([values, values], axis=1)
            result = total[:, index * LANES:(index + 1) * LANES] + jnp.dot(
                twice, z_weights[...], preferred_element_type=f32
            )
            corner = corners[first + index]
            window = flat[pl.ds(corner // 2, TILES + 1)].astype(f32).reshape(ROWS + TILE, LANES)
            local = jnp.where(corner % 2 == 1, window[8:8 + ROWS], window[:ROWS])
            term = (local * values.astype(f32)).astype(bf16).astype(f32)
            out[first + index] = (result + term).astype(bf16)
        copy = pltpu.make_async_copy(
            out.at[pl.ds(first, 2)], applied.at[pl.ds(first, 2)], out_sem.at[pair]
        )
        copy.start()
        loads["out", pair] = copy

    loads["potential"].wait()
    gathered[x, z, core] = pot_in[...].astype(bf16).reshape(TILES, TILE, LANES)
    gather_step(0)
    for pair in range(PAIRS):
        where = pl.ds(2 * pair, 2)
        send(("halo", pair, 0), support.at[where], left.at[where], y_next)
        send(("halo", pair, 1), support.at[where], right.at[where], y_prev)

    bases = [corners[k] // 32 for k in range(FUNCS)]

    def find(block, carry):
        found = FUNCS
        for k in reversed(range(FUNCS)):
            found = jnp.where(bases[k] == block, k, found)
        table[block] = found * PLANES
        return carry

    lax.fori_loop(0, 64, find, 0)
    terms[pl.ds(FUNCS * PLANES, PLANES)] = jnp.zeros((PLANES, 8, LANES), f32)
    loads["support"].wait()
    for k in range(FUNCS):
        value = own[k].astype(f32)
        twin = k
        for other in reversed(range(k + 1, FUNCS)):
            twin = jnp.where(bases[other] == bases[k], other, twin)
        total = occupation[k] * value * value
        if k + 1 < FUNCS:
            second = own[twin].astype(f32)
            weight = jnp.where(twin == k, 0.0, occupation[twin])
            total = total + weight * second * second
        terms[pl.ds(k * PLANES, PLANES)] = total.reshape(PLANES, 8, LANES)
    gather_step(1)
    for dz in levels[0] + levels[1]:
        build_partner(dz)
    gather_step(2)
    build_own(4)
    scatter_step(0)
    for level in range(1, 5):
        if level < 4:
            for dz in levels[level + 1]:
                build_partner(dz)
        for dz in levels[level]:
            build_own(dz)
        scatter_step(level)
        if level < 4:
            gather_step(level + 2)
    gather_step(6)
    scatter_step(5)
    gather_end()
    loads["rows"].wait()
    loads["z"].wait()
    for pair in range(3):
        apply(pair)
    scatter_step(6)
    scatter_end()
    for pair in range(3, PAIRS):
        apply(pair)
    for copy in sent.values():
        copy.wait_send()
    for pair in range(PAIRS):
        loads["out", pair].wait()
    loads["density"].wait()


def on_device(support, corners, occupation, potential):
    rows, z_mix = stencil_matrices()
    bf16, f32 = jnp.bfloat16, jnp.float32
    vmem = lambda shape, kind=bf16: pltpu.VMEM(shape, kind)
    smem = pl.BlockSpec(memory_space=pltpu.SMEM)
    anywhere = pl.BlockSpec(memory_space=pl.ANY)
    copies = 160
    applied, density = pl.pallas_call(
        kernel,
        out_shape=(
            jax.ShapeDtypeStruct((FUNCS, ROWS, LANES), bf16),
            jax.ShapeDtypeStruct((ROWS, LANES), f32),
        ),
        in_specs=[smem, smem, anywhere, anywhere, anywhere, anywhere],
        out_specs=(anywhere, anywhere),
        scratch_shapes=[
            vmem((FUNCS, ROWS, LANES)),
            vmem((FUNCS, ROWS, LANES)),
            vmem((FUNCS, ROWS, LANES)),
            vmem((FUNCS, ROWS, LANES)),
            vmem((ROWS, LANES), f32),
            vmem((ROWS, LANES), f32),
            vmem(rows.shape),
            vmem(z_mix.shape),
            vmem((NXC + 1, NZC, 2, TILES, TILE, LANES)),
            vmem(((FUNCS + 1) * PLANES, 8, LANES), f32),
            pltpu.SMEM((64,), jnp.int32),
            vmem((NZC, NXC, ROWS, LANES)),
            vmem((NZC, NXC, ROWS, LANES)),
            vmem((NZC, NXC, ROWS, LANES)),
            vmem((NZC, 2, HA, LANES)),
            vmem((NZC, 2, RA, LANES)),
            vmem((2, HA, LANES)),
            vmem((3, 2, RA, LANES)),
            vmem((2, NXC, HB, LANES)),
            vmem((3, 2, NXC, RB, LANES)),
            vmem((2, HB, LANES)),
            vmem((2, RB, LANES)),
            pltpu.SemaphoreType.DMA((4,)),
            pltpu.SemaphoreType.DMA((PAIRS + 1,)),
            pltpu.SemaphoreType.DMA((copies,)),
            pltpu.SemaphoreType.DMA((copies,)),
        ],
        compiler_params=pltpu.CompilerParams(
            collective_id=0, has_side_effects=True, vmem_limit_bytes=48 * 1024 * 1024
        ),
    )(
        corners,
        occupation.astype(f32),
        support.reshape(FUNCS, ROWS, LANES),
        potential.reshape(ROWS, LANES),
        jnp.asarray(rows),
        jnp.asarray(z_mix),
    )
    return applied.reshape(support.shape), density.reshape(potential.shape)


def solution(mesh):
    in_specs = (P("grp", None, "slab", None), P("grp"), P("grp"), P("grp", "slab", None))
    out_specs = (P("grp", None, "slab", None), P("grp", "slab", None))
    return jax.shard_map(
        on_device, mesh=mesh, in_specs=in_specs, out_specs=out_specs, check_vma=False
    )
```

```python
import functools
import math

import jax
import jax.numpy as jnp
import numpy as np
from jax import lax
from jax.experimental import pallas as pl
from jax.experimental.pallas import tpu as pltpu
from jax.sharding import PartitionSpec as P

MESH = pl.DeviceIdType.MESH
FUNCS, ROWS, LANES = 16, 256, 128
NXC, NZC = 4, 8
PAIRS = FUNCS // 2
TILE = 16
PLANES, TILES = ROWS // 8, ROWS // TILE
RA = 160
RB = ROWS - RA
HA, HB = RA // 2, RB // 2

kinetic_taps = [
    2.0 * (-1.0) ** (index + 2) / float((index + 1) * (index + 1)) for index in range(8)
]
center_tap = -math.pi * math.pi / 3.0


ORDER = (
    ("bx1",), ("az", 1, 0), ("az", 1, 1), ("bpart", 4), ("ax1", 0), ("halo",), ("bpart", 5), ("bx2", 0),
    ("bx2", 1), ("bown", 4), ("rax1", 4), ("rbz", 2, 1), ("ax1", 7), ("az", 2, 1), ("bpart", 3), ("az", 2, 0),
    ("rbz", 0, 1), ("rbz", 3, 1), ("bpart", 2), ("ax1", 1), ("bown", 5), ("rax1", 5), ("rbz", 1, 1),
    ("bpart", 6), ("bown", 3), ("rax1", 3), ("bz", 1, 1), ("bz", 1, 0), ("ax2", 0, 0), ("ax2", 0, 1),
    ("rbz", 2, 2, 0), ("rax2", 4, 1), ("rax2", 4, 0), ("bown", 2), ("bpart", 7), ("rax1", 2),
    ("rbz", 2, 2, 1), ("bown", 6), ("bpart", 0), ("az", 3, 1), ("az", 3, 0), ("rax1", 6), ("ax1", 6),
    ("bpart", 1), ("ax2", 1, 0), ("rbz", 1, 2, 0), ("rax2", 3, 1), ("rbz", 3, 2, 0), ("rbz", 3, 2, 1),
    ("rax2", 3, 0), ("rbz", 1, 2, 1), ("rbz", 0, 2, 0), ("ax2", 1, 1), ("bown", 0), ("rax2", 5, 0),
    ("ax1", 2), ("rax2", 5, 1), ("ax2", 7, 1), ("rbz", 0, 2, 1), ("bown", 7), ("rax1", 7), ("rax3", 4),
    ("raz", 1), ("rbz", 2, 3, 0), ("rbz", 2, 3, 1), ("rax2", 2, 1), ("rax2", 6, 0), ("bz", 2, 1),
    ("bz", 2, 0), ("bown", 1), ("rax1", 1), ("lap", 2), ("rbz", 1, 3, 1), ("rax3", 3), ("rax2", 2, 0),
    ("az", 4, 0), ("ax2", 6, 0), ("az", 4, 1), ("raz", 2, 0), ("rax2", 6, 1), ("rbz", 1, 3, 0),
    ("rbz", 2, 4, 1), ("lap", 0), ("ax1", 5), ("rbz", 2, 4, 0), ("rbz", 3, 3, 0), ("ax2", 6, 1),
    ("rbz", 3, 3, 1), ("lap", 3), ("rax3", 5), ("ax2", 2, 1), ("raz", 2, 1), ("ax1", 3), ("bz", 3, 1),
    ("ax2", 7, 0), ("rbz", 0, 3, 1), ("bp", 0), ("bz", 3, 0), ("rax2", 7, 0), ("bp", 2, 0), ("ax1", 4),
    ("rbz", 1, 4, 1), ("rax1", 0), ("rbz", 0, 3, 0), ("rax2", 1, 0), ("ap", 1), ("ax2", 2, 0), ("rax2", 7, 1),
    ("rax3", 2), ("raz", 3, 0), ("rax3", 6), ("raz", 3, 1), ("rbz", 1, 4, 0), ("rbz", 3, 4, 0),
    ("rax2", 1, 1), ("rbx1",), ("bp", 1, 0), ("ax2", 5, 0), ("ax2", 5, 1), ("rbz", 3, 4, 1), ("lap", 1),
    ("ax2", 3, 0), ("bp", 3, 0), ("ax2", 3, 1), ("bz", 4, 0), ("bz", 4, 1), ("ax2", 4, 0), ("ap", 0),
    ("ax2", 4, 1), ("bp", 2, 1), ("ap", 6), ("rbz", 0, 4, 0), ("rbz", 0, 4, 1), ("rax2", 0, 1),
    ("rax2", 0, 0), ("rax3", 7), ("raz", 4, 1), ("ap", 7), ("ap", 2), ("rax3", 1), ("raz", 4, 0), ("rbx2", 1),
    ("bp", 1, 1), ("rbx2", 0), ("ap", 5), ("lap", 4), ("bp", 3, 1), ("ap", 3), ("ap", 4), ("bp", 4),
    ("lap", 5), ("rax3", 0), ("lap", 6), ("lap", 7), ("agend",), ("fin", 6), ("fin", 0), ("fin", 3),
    ("fin", 2), ("fin", 1), ("fin", 7), ("fin", 4), ("fin", 5), ("rsend",),
)


def split_bf16(matrix):
    high = matrix.astype(jnp.bfloat16)
    low = (matrix - high.astype(np.float64)).astype(jnp.bfloat16)
    return high, low


def stencil_matrices():
    along_y, along_x = np.zeros((32, 32)), np.zeros((8, 8))
    left, right, along_z = np.zeros((8, 8)), np.zeros((8, 8)), np.zeros((LANES, LANES))
    for offset in range(1, 9):
        weight = kinetic_taps[offset - 1]
        along_y += weight * (np.eye(32, k=offset) + np.eye(32, k=-offset))
        along_x += weight * (np.eye(8, k=offset) + np.eye(8, k=-offset))
        left += weight * np.eye(8, k=8 - offset)
        right += weight * np.eye(8, k=offset - 8)
        along_z += weight * (
            np.roll(np.eye(LANES), offset, 1) + np.roll(np.eye(LANES), -offset, 1)
        )
    own = (
        np.kron(along_y, np.eye(8))
        + np.kron(np.eye(32), along_x)
        + 3.0 * center_tap * np.eye(ROWS)
    )
    rows = np.concatenate(
        [own, np.kron(np.eye(32), left), np.kron(np.eye(32), right)], axis=1
    )
    rows_high, rows_low = split_bf16(-0.5 * rows)
    z_high, z_low = split_bf16(-0.5 * along_z)
    halves = [part[:, at:at + LANES] for part in (rows_high, rows_low) for at in range(0, 3 * ROWS, LANES)]
    mixes = np.stack([*halves, np.concatenate([z_high, z_low], axis=0)])
    return mixes.reshape(len(mixes), PLANES, 8, LANES)


def kernel(
    corners, occupation, support, potential, mixes_in,
    applied, density,
    own, left, right, out, pot_in, dens, mixes,
    kinetic, gathered, terms, table, part_out, part_in, sums,
    xa1, xa2, za1, za, zb1, zb, xb1, xb2,
    load_sem, out_sem, send_sem, recv_sem,
):
    f32, bf16 = jnp.float32, jnp.bfloat16
    group, slab = lax.axis_index("grp"), lax.axis_index("slab")
    x, z, core = group // 16, (group // 2) % 8, group % 2

    def chip(dx, dz):
        return ((((x + dx) % NXC) * NZC + (z + dz) % NZC) * 2 + core, slab)

    partner = (group + 1 - 2 * core, slab)
    x_next, x_prev = chip(1, 0), chip(NXC - 1, 0)
    z_next, z_prev = chip(0, 1), chip(0, NZC - 1)
    y_next, y_prev = (group, (slab + 1) % 4), (group, (slab + 3) % 4)
    along_x, along_z, along_y = (x_next, x_prev), (z_next, z_prev), (y_next, y_prev)

    loads = {}
    for index, (name, src, dst) in enumerate([
        ("potential", potential, pot_in),
        ("support", support, own),
        ("mixes", mixes_in.reshape(mixes.shape), mixes),
    ]):
        loads[name] = pltpu.make_async_copy(src, dst, load_sem.at[index])
        loads[name].start()

    sent, pending = {}, set()

    def send(name, src, dst, device):
        index = len(sent)
        copy = pltpu.make_async_remote_copy(
            src_ref=src, dst_ref=dst,
            send_sem=send_sem.at[index], recv_sem=recv_sem.at[index],
            device_id=device, device_id_type=MESH,
        )
        copy.start()
        sent[name] = copy
        pending.add(name)

    barrier = pltpu.get_barrier_semaphore()
    neighbours = (*along_x, *along_z, *along_y, partner)
    for device in neighbours:
        pl.semaphore_signal(barrier, inc=1, device_id=device, device_id_type=MESH)

    def arrived(*name):
        if name in pending:
            pending.remove(name)
            sent[name].wait_recv()

    def slot(dx, dz, start, size):
        tiles = pl.ds(start // TILE, size // TILE)
        return gathered.at[(x + dx) % NXC, (z + dz) % NZC, core, tiles]

    def column(dz, start, size):
        tiles = pl.ds(start // TILE, size // TILE)
        return gathered.at[pl.ds(0, NXC), (z + dz) % NZC, core, tiles]

    def from_way(way, distance):
        return (NZC - distance) % NZC if way == 0 else distance

    def az(step, way):
        if step > 1:
            arrived("az", step - 1, way)
        dz = from_way(way, step - 1)
        where = slot(0, dz, 0, RA) if step < 4 else slot(0, dz, way * HA, HA)
        send(("az", step, way), where, where, along_z[way])

    def ax1(dz):
        if dz == 4:
            arrived("az", 4, 0)
            arrived("az", 4, 1)
        elif dz:
            arrived("az", min(dz, NZC - dz), 0 if dz > 4 else 1)
        for way in range(2):
            where = slot(0, dz, 0, RA)
            send(("ax1", dz, way), where, where, along_x[way])

    def ax2(dz, way):
        arrived("ax1", dz, way)
        where = slot(3 if way == 0 else 1, dz, way * HA, HA)
        send(("ax2", dz, way), where, where, along_x[way])

    def ap(dz):
        for way in range(2):
            arrived("ax2", dz, way)
        where = column(dz, 0, RA)
        send(("ap", dz), where, where, partner)

    def bx1():
        for way in range(2):
            where = slot(0, 0, RA, RB)
            send(("bx1", way), where, where, along_x[way])

    def bx2(way):
        arrived("bx1", way)
        where = slot(3 if way == 0 else 1, 0, RA + way * HB, HB)
        send(("bx2", way), where, where, along_x[way])

    def bz(step, way):
        if step == 1:
            arrived("bx2", 0)
            arrived("bx2", 1)
        else:
            arrived("bz", step - 1, way)
        dz = from_way(way, step - 1)
        where = column(dz, RA, RB) if step < 4 else column(dz, RA + way * HB, HB)
        send(("bz", step, way), where, where, along_z[way])

    def bp(distance, way=0):
        if distance == 0:
            arrived("bx2", 0)
            arrived("bx2", 1)
        elif distance == 4:
            arrived("bz", 4, 0)
            arrived("bz", 4, 1)
        else:
            arrived("bz", distance, way)
        dz = from_way(way, distance)
        where = column(dz, RA, RB)
        send(("bp", dz), where, where, partner)

    def agend():
        for dz in range(NZC):
            arrived("ap", dz)
            arrived("bp", dz)
        gathered[4, 0, 0] = gathered[0, 0, 0]

    def build(target, dz, owner, added=None):
        shift = corners[0] % PLANES

        def one(dx, carry):
            block = ((x + dx) % NXC) * 16 + ((z + dz) % NZC) * 2 + owner
            after = table[block] - shift
            before = table[(block + 63) % 64] + PLANES - shift
            for at in range(0, PLANES, 2):
                planes = [
                    terms[plane + jnp.where(plane >= shift, after, before)]
                    for plane in (at, at + 1)
                ]
                value = jnp.concatenate(planes, axis=0)
                rows = pl.ds(at * 8, TILE)
                if added is not None:
                    value = value + added[dz, dx, rows, :].astype(f32)
                target[dz, dx, rows, :] = value.astype(bf16)
            return carry

        lax.fori_loop(0, NXC, one, 0)

    def bpart(dz):
        build(part_out, dz, 1 - core)
        send(("part", dz), part_out.at[dz], part_in.at[dz], partner)

    def bown(dz):
        arrived("part", dz)
        build(sums, dz, core, part_in)

    def add(where, start, size, *others):
        total = where[pl.ds(start, size), :].astype(f32)
        for other in others:
            total = total + other[...].astype(f32)
        where[pl.ds(start, size), :] = total.astype(bf16)

    def rax1(dz):
        for way in range(2):
            part = sums.at[dz, 2, pl.ds(way * HA, HA)]
            send(("rax1", dz, way), part, xa1.at[dz, way], along_x[way])

    def rax2(dz, way):
        dx = 1 if way == 0 else 3
        arrived("rax1", dz, way)
        add(sums.at[dz, dx], way * HA, HA, xa1.at[dz, way])
        part = sums.at[dz, dx, pl.ds(0, RA)]
        send(("rax2", dz, way), part, xa2.at[dz, way], along_x[way])

    def rax3(dz):
        for way in range(2):
            arrived("rax2", dz, way)
        add(sums.at[dz, 0], 0, RA, xa2.at[dz, 0], xa2.at[dz, 1])

    def raz(step, way=None):
        if step == 1:
            for way in range(2):
                part = sums.at[4, 0, pl.ds(way * HA, HA)]
                send(("raz", 1, way), part, za1.at[way], along_z[way])
            return
        dz = 5 - step if way == 0 else 3 + step
        arrived("raz", step - 1, way)
        if step == 2:
            add(sums.at[dz, 0], way * HA, HA, za1.at[way])
        else:
            add(sums.at[dz, 0], 0, RA, za.at[step - 3, way])
        part = sums.at[dz, 0, pl.ds(0, RA)]
        send(("raz", step, way), part, za.at[step - 2, way], along_z[way])

    def rbz(dx, step, way=None):
        if step == 1:
            for way in range(2):
                part = sums.at[4, dx, pl.ds(RA + way * HB, HB)]
                send(("rbz", dx, 1, way), part, zb1.at[way, dx], along_z[way])
            return
        dz = 5 - step if way == 0 else 3 + step
        arrived("rbz", dx, step - 1, way)
        if step == 2:
            add(sums.at[dz, dx], RA + way * HB, HB, zb1.at[way, dx])
        else:
            add(sums.at[dz, dx], RA, RB, zb.at[step - 3, way, dx])
        part = sums.at[dz, dx, pl.ds(RA, RB)]
        send(("rbz", dx, step, way), part, zb.at[step - 2, way, dx], along_z[way])

    def rbz_end(dx):
        for way in range(2):
            arrived("rbz", dx, 4, way)
        add(sums.at[0, dx], RA, RB, zb.at[2, 0, dx], zb.at[2, 1, dx])

    def rbx1():
        rbz_end(2)
        for way in range(2):
            part = sums.at[0, 2, pl.ds(RA + way * HB, HB)]
            send(("rbx1", way), part, xb1.at[way], along_x[way])

    def rbx2(way):
        dx = 1 if way == 0 else 3
        rbz_end(dx)
        arrived("rbx1", way)
        add(sums.at[0, dx], RA + way * HB, HB, xb1.at[way])
        send(("rbx2", way), sums.at[0, dx, pl.ds(RA, RB)], xb2.at[way], along_x[way])

    def rsend():
        for way in range(2):
            arrived("raz", 4, way)
            for dx in range(NXC):
                arrived("rbz", dx, 4, way)
            arrived("rbx2", way)
        dens[pl.ds(0, RA), :] = (
            sums[0, 0, pl.ds(0, RA), :].astype(f32)
            + za[2, 0].astype(f32) + za[2, 1].astype(f32)
        )
        dens[pl.ds(RA, RB), :] = (
            sums[0, 0, pl.ds(RA, RB), :].astype(f32)
            + zb[2, 0, 0].astype(f32) + zb[2, 1, 0].astype(f32)
            + xb2[0].astype(f32) + xb2[1].astype(f32)
        )
        loads["density"] = pltpu.make_async_copy(dens, density, out_sem.at[PAIRS])
        loads["density"].start()

    def halo():
        for pair in range(PAIRS):
            where = pl.ds(2 * pair, 2)
            send(("halo", pair, 0), support.at[where], left.at[where], y_next)
            send(("halo", pair, 1), support.at[where], right.at[where], y_prev)

    def lap(pair):
        if pair == first_lap:
            loads["mixes"].wait()
        arrived("halo", pair, 0)
        arrived("halo", pair, 1)
        first = 2 * pair
        cells = jnp.concatenate([
            jnp.concatenate([ref[first], ref[first + 1]], axis=1) for ref in (own, left, right)
        ], axis=0)
        high, low = (
            jnp.concatenate([mixes[at + piece] for piece in range(6)], axis=1) for at in (0, 6)
        )
        total = jnp.dot(high, cells, preferred_element_type=f32)
        total = total + jnp.dot(low, cells, preferred_element_type=f32)
        for index in range(2):
            values = own[first + index]
            twice = jnp.concatenate([values, values], axis=1)
            kinetic[first + index] = total[:, index * LANES:(index + 1) * LANES] + jnp.dot(
                twice, mixes[12], preferred_element_type=f32
            )

    def fin(pair):
        first = 2 * pair
        flat = gathered.reshape(5 * NZC * 2 * TILES, TILE, LANES)
        for func in (first, first + 1):
            corner = corners[func]
            window = flat[pl.ds(corner // 2, TILES + 1)].astype(f32).reshape(ROWS + TILE, LANES)
            local = jnp.where(corner % 2 == 1, window[8:8 + ROWS], window[:ROWS])
            term = (local * own[func].astype(f32)).astype(bf16).astype(f32)
            out[func] = (kinetic[func] + term).astype(bf16)
        loads["out", pair] = pltpu.make_async_copy(
            out.at[pl.ds(first, 2)], applied.at[pl.ds(first, 2)], out_sem.at[pair]
        )
        loads["out", pair].start()

    bases = [corners[k] // 32 for k in range(FUNCS)]

    def find(block, carry):
        found = FUNCS
        for k in reversed(range(FUNCS)):
            found = jnp.where(bases[k] == block, k, found)
        table[block] = found * PLANES
        return carry

    lax.fori_loop(0, 64, find, 0)
    terms[pl.ds(FUNCS * PLANES, PLANES)] = jnp.zeros((PLANES, 8, LANES), f32)
    loads["potential"].wait()
    gathered[x, z, core] = pot_in[...].astype(bf16).reshape(TILES, TILE, LANES)
    loads["support"].wait()
    for k in range(FUNCS):
        value = own[k].astype(f32)
        twin = k
        for other in reversed(range(k + 1, FUNCS)):
            twin = jnp.where(bases[other] == bases[k], other, twin)
        total = occupation[k] * value * value
        if k + 1 < FUNCS:
            second = own[twin].astype(f32)
            weight = jnp.where(twin == k, 0.0, occupation[twin])
            total = total + weight * second * second
        terms[pl.ds(k * PLANES, PLANES)] = total.reshape(PLANES, 8, LANES)
    pl.semaphore_wait(barrier, len(neighbours))

    steps = {step.__name__: step for step in (
        az, ax1, ax2, ap, bx1, bx2, bz, bp, agend, bpart, bown, rax1, rax2, rax3,
        raz, rbz, rbx1, rbx2, rsend, halo, lap, fin,
    )}
    first_lap = next(args[0] for name, *args in ORDER if name == "lap")
    for name, *args in ORDER:
        steps[name](*args)
    for copy in sent.values():
        copy.wait_send()
    for pair in range(PAIRS):
        loads["out", pair].wait()
    loads["density"].wait()


def on_device(support, corners, occupation, potential):
    mixes = stencil_matrices()
    bf16, f32 = jnp.bfloat16, jnp.float32
    vmem = lambda shape, kind=bf16: pltpu.VMEM(shape, kind)
    smem = pl.BlockSpec(memory_space=pltpu.SMEM)
    anywhere = pl.BlockSpec(memory_space=pl.ANY)
    copies = 192
    applied, density = pl.pallas_call(
        kernel,
        out_shape=(
            jax.ShapeDtypeStruct((FUNCS, ROWS, LANES), bf16),
            jax.ShapeDtypeStruct((ROWS, LANES), f32),
        ),
        in_specs=[smem, smem, anywhere, anywhere, anywhere],
        out_specs=(anywhere, anywhere),
        scratch_shapes=[
            vmem((FUNCS, ROWS, LANES)),
            vmem((FUNCS, ROWS, LANES)),
            vmem((FUNCS, ROWS, LANES)),
            vmem((FUNCS, ROWS, LANES)),
            vmem((ROWS, LANES), f32),
            vmem((ROWS, LANES), f32),
            vmem((len(mixes), ROWS, LANES)),
            vmem((FUNCS, ROWS, LANES), f32),
            vmem((NXC + 1, NZC, 2, TILES, TILE, LANES)),
            vmem(((FUNCS + 1) * PLANES, 8, LANES), f32),
            pltpu.SMEM((64,), jnp.int32),
            vmem((NZC, NXC, ROWS, LANES)),
            vmem((NZC, NXC, ROWS, LANES)),
            vmem((NZC, NXC, ROWS, LANES)),
            vmem((NZC, 2, HA, LANES)),
            vmem((NZC, 2, RA, LANES)),
            vmem((2, HA, LANES)),
            vmem((3, 2, RA, LANES)),
            vmem((2, NXC, HB, LANES)),
            vmem((3, 2, NXC, RB, LANES)),
            vmem((2, HB, LANES)),
            vmem((2, RB, LANES)),
            pltpu.SemaphoreType.DMA((4,)),
            pltpu.SemaphoreType.DMA((PAIRS + 1,)),
            pltpu.SemaphoreType.DMA((copies,)),
            pltpu.SemaphoreType.DMA((copies,)),
        ],
        compiler_params=pltpu.CompilerParams(
            collective_id=0, has_side_effects=True, vmem_limit_bytes=60 * 1024 * 1024
        ),
    )(
        corners,
        occupation.astype(f32),
        support.reshape(FUNCS, ROWS, LANES),
        potential.reshape(ROWS, LANES),
        jnp.asarray(mixes),
    )
    return applied.reshape(support.shape), density.reshape(potential.shape)


def solution(mesh):
    in_specs = (P("grp", None, "slab", None), P("grp"), P("grp"), P("grp", "slab", None))
    out_specs = (P("grp", None, "slab", None), P("grp", "slab", None))
    return jax.shard_map(
        on_device, mesh=mesh, in_specs=in_specs, out_specs=out_specs, check_vma=False
    )
```

```python
import functools
import math

import jax
import jax.numpy as jnp
import numpy as np
from jax import lax
from jax.experimental import pallas as pl
from jax.experimental.pallas import tpu as pltpu
from jax.sharding import PartitionSpec as P

MESH = pl.DeviceIdType.MESH
FUNCS, ROWS, LANES = 16, 256, 128
NXC, NZC = 4, 8
PAIRS = FUNCS // 2
TILE = 16
PLANES, TILES = ROWS // 8, ROWS // TILE
RA = 160
RB = ROWS - RA
HA, HB = RA // 2, RB // 2
SENT_ROWS = 40448

kinetic_taps = [
    2.0 * (-1.0) ** (index + 2) / float((index + 1) * (index + 1)) for index in range(8)
]
center_tap = -math.pi * math.pi / 3.0


ORDER = (
    ("az", 1, 1), ("bx1",), ("az", 1, 0), ("bpart", 4), ("ax1", 0), ("bpart", 5), ("halo",), ("bpart", 3),
    ("bown", 4), ("rax1", 4), ("rbz", 1, 1), ("bown", 5), ("rax1", 5), ("rbz", 2, 1), ("bx2", 0), ("bx2", 1),
    ("ax1", 1), ("az", 2, 0), ("az", 2, 1), ("bown", 3), ("rax1", 3), ("rbz", 0, 1), ("bpart", 6), ("ax1", 7),
    ("ax2", 0, 1), ("bpart", 2), ("rbz", 3, 1), ("rbz", 1, 2, 0), ("rbz", 1, 2, 1), ("rax2", 4, 0),
    ("rax2", 4, 1), ("rbz", 2, 2, 1), ("rbz", 2, 2, 0), ("bz", 1, 1), ("bz", 1, 0), ("ax2", 0, 0),
    ("bown", 2), ("rax1", 2), ("bown", 6), ("rax1", 6), ("rax2", 5, 1), ("az", 3, 0), ("rax2", 5, 0),
    ("bpart", 7), ("rbz", 3, 2, 0), ("rbz", 3, 2, 1), ("rax2", 3, 1), ("rax2", 3, 0), ("az", 3, 1),
    ("ax1", 6), ("rbz", 2, 3, 0), ("ax1", 2), ("rbz", 0, 2, 1), ("rax3", 4), ("raz", 1), ("bown", 7),
    ("bpart", 1), ("rbz", 2, 3, 1), ("rbz", 0, 2, 0), ("rax2", 6, 1), ("rax1", 7), ("rax2", 6, 0),
    ("rax2", 2, 0), ("bz", 2, 1), ("bz", 2, 0), ("rbz", 1, 3, 1), ("rax3", 5), ("bpart", 0), ("ax2", 1, 1),
    ("ax2", 7, 1), ("az", 4, 0), ("ax2", 1, 0), ("az", 4, 1), ("bown", 1), ("rax2", 2, 1), ("rbz", 1, 3, 0),
    ("rbz", 3, 3, 1), ("bown", 0), ("rax1", 0), ("rax1", 1), ("rbz", 2, 4, 0), ("rbz", 3, 3, 0),
    ("rbz", 2, 4, 1), ("ax2", 7, 0), ("ap", 0), ("raz", 2, 1), ("ax2", 6, 1), ("ax2", 2, 1), ("ax1", 5),
    ("ax2", 2, 0), ("rax3", 3), ("raz", 2, 0), ("ax1", 3), ("bz", 3, 1), ("bz", 3, 0), ("rax3", 6),
    ("bp", 1, 1), ("lap", 2), ("ax1", 4), ("bp", 2, 1), ("rax2", 7, 1), ("ax2", 6, 0), ("lap", 0),
    ("rbz", 0, 3, 1), ("rax2", 1, 1), ("rbz", 0, 3, 0), ("rbz", 3, 4, 1), ("rax2", 7, 0), ("lap", 3),
    ("rbz", 1, 4, 0), ("ap", 1), ("raz", 3, 1), ("rax2", 1, 0), ("rax3", 2), ("raz", 3, 0), ("rbx1",),
    ("rbz", 3, 4, 0), ("ax2", 5, 1), ("rbz", 1, 4, 1), ("ax2", 5, 0), ("ax2", 3, 0), ("ap", 7), ("ax2", 3, 1),
    ("bz", 4, 1), ("bz", 4, 0), ("ax2", 4, 0), ("bp", 1, 0), ("ax2", 4, 1), ("rax2", 0, 1), ("rax2", 0, 0),
    ("bp", 0), ("rbz", 0, 4, 1), ("lap", 5), ("bp", 3, 0), ("rbz", 0, 4, 0), ("ap", 2), ("ap", 6),
    ("rax3", 7), ("bp", 3, 1), ("bp", 2, 0), ("raz", 4, 1), ("rax3", 1), ("raz", 4, 0), ("rbx2", 0),
    ("rbx2", 1), ("ap", 5), ("ap", 3), ("lap", 1), ("ap", 4), ("bp", 4), ("lap", 4), ("lap", 6), ("rax3", 0),
    ("lap", 7), ("agend",), ("fin", 1), ("fin", 5), ("fin", 0), ("fin", 4), ("fin", 3), ("fin", 2),
    ("fin", 6), ("fin", 7), ("rsend",),
)


def split_bf16(matrix):
    high = matrix.astype(jnp.bfloat16)
    low = (matrix - high.astype(np.float64)).astype(jnp.bfloat16)
    return high, low


def stencil_matrices():
    along_y, along_x = np.zeros((32, 32)), np.zeros((8, 8))
    left, right, along_z = np.zeros((8, 8)), np.zeros((8, 8)), np.zeros((LANES, LANES))
    for offset in range(1, 9):
        weight = kinetic_taps[offset - 1]
        along_y += weight * (np.eye(32, k=offset) + np.eye(32, k=-offset))
        along_x += weight * (np.eye(8, k=offset) + np.eye(8, k=-offset))
        left += weight * np.eye(8, k=8 - offset)
        right += weight * np.eye(8, k=offset - 8)
        along_z += weight * (
            np.roll(np.eye(LANES), offset, 1) + np.roll(np.eye(LANES), -offset, 1)
        )
    own = (
        np.kron(along_y, np.eye(8))
        + np.kron(np.eye(32), along_x)
        + 3.0 * center_tap * np.eye(ROWS)
    )
    rows = np.concatenate(
        [own, np.kron(np.eye(32), left), np.kron(np.eye(32), right)], axis=1
    )
    rows_high, rows_low = split_bf16(-0.5 * rows)
    z_high, z_low = split_bf16(-0.5 * along_z)
    halves = [part[:, at:at + LANES] for part in (rows_high, rows_low) for at in range(0, 3 * ROWS, LANES)]
    mixes = np.stack([*halves, np.concatenate([z_high, z_low], axis=0)])
    return mixes.reshape(len(mixes), PLANES, 8, LANES)


def kernel(
    corners_in, occupation_in, support, potential, mixes_in,
    applied, density,
    corners, occupation, weights, own, left, right, out, pot_in, dens, mixes,
    kinetic, gathered, terms, table, part_out, part_in, sums,
    xa1, xa2, za1, za, zb1, zb, xb1, xb2, tally,
    load_sem, out_sem, send_sem, recv_sem,
):
    f32, bf16 = jnp.float32, jnp.bfloat16
    group, slab = lax.axis_index("grp"), lax.axis_index("slab")
    x, z, core = group // 16, (group // 2) % 8, group % 2

    def chip(dx, dz):
        return ((((x + dx) % NXC) * NZC + (z + dz) % NZC) * 2 + core, slab)

    partner = (group + 1 - 2 * core, slab)
    x_next, x_prev = chip(1, 0), chip(NXC - 1, 0)
    z_next, z_prev = chip(0, 1), chip(0, NZC - 1)
    y_next, y_prev = (group, (slab + 1) % 4), (group, (slab + 3) % 4)
    along_x, along_z, along_y = (x_next, x_prev), (z_next, z_prev), (y_next, y_prev)

    loads = {}
    for index, (name, src, dst) in enumerate([
        ("corners", corners_in, corners),
        ("potential", potential, pot_in),
        ("occupation", occupation_in, occupation),
        ("support", support, own),
        ("mixes", mixes_in.reshape(mixes.shape), mixes),
    ]):
        loads[name] = pltpu.make_async_copy(src, dst, load_sem.at[index])
        loads[name].start()

    slots, pending, rows = {}, {}, []

    def send(name, src, dst, device):
        index = slots.setdefault(name, len(slots))
        rows.append(math.prod(src.shape[:-1]))
        pending[name] = pending.get(name, 0) + rows[-1]
        pltpu.make_async_remote_copy(
            src_ref=src, dst_ref=dst,
            send_sem=send_sem, recv_sem=recv_sem.at[index],
            device_id=device, device_id_type=MESH,
        ).start()

    barrier = pltpu.get_barrier_semaphore()
    neighbours = (*along_x, *along_z, *along_y, partner)
    for device in neighbours:
        pl.semaphore_signal(barrier, inc=1, device_id=device, device_id_type=MESH)

    def arrived(*name):
        if name in pending:
            whole = tally.at[pl.ds(0, pending.pop(name))]
            pltpu.make_async_copy(whole, whole, recv_sem.at[slots[name]]).wait()

    def slot(dx, dz, start, size):
        tiles = pl.ds(start // TILE, size // TILE)
        return gathered.at[(x + dx) % NXC, (z + dz) % NZC, core, tiles]

    def column(dz, start, size):
        tiles = pl.ds(start // TILE, size // TILE)
        return gathered.at[pl.ds(0, NXC), (z + dz) % NZC, core, tiles]

    def from_way(way, distance):
        return (NZC - distance) % NZC if way == 0 else distance

    def az(step, way):
        if step > 1:
            arrived("az", step - 1, way)
        dz = from_way(way, step - 1)
        where = slot(0, dz, 0, RA) if step < 4 else slot(0, dz, way * HA, HA)
        send(("az", 4) if step == 4 else ("az", step, way), where, where, along_z[way])

    def ax1(dz):
        if dz == 4:
            arrived("az", 4)
        elif dz:
            arrived("az", min(dz, NZC - dz), 0 if dz > 4 else 1)
        for way in range(2):
            where = slot(0, dz, 0, RA)
            send(("ax1", dz, way), where, where, along_x[way])

    def ax2(dz, way):
        arrived("ax1", dz, way)
        where = slot(3 if way == 0 else 1, dz, way * HA, HA)
        send(("ax2", dz), where, where, along_x[way])

    def ap(dz):
        arrived("ax2", dz)
        where = column(dz, 0, RA)
        send(("ap",), where, where, partner)

    def bx1():
        for way in range(2):
            where = slot(0, 0, RA, RB)
            send(("bx1", way), where, where, along_x[way])

    def bx2(way):
        arrived("bx1", way)
        where = slot(3 if way == 0 else 1, 0, RA + way * HB, HB)
        send(("bx2",), where, where, along_x[way])

    def bz(step, way):
        if step == 1:
            arrived("bx2")
        else:
            arrived("bz", step - 1, way)
        dz = from_way(way, step - 1)
        where = column(dz, RA, RB) if step < 4 else column(dz, RA + way * HB, HB)
        send(("bz", 4) if step == 4 else ("bz", step, way), where, where, along_z[way])

    def bp(distance, way=0):
        if distance == 0:
            arrived("bx2")
        elif distance == 4:
            arrived("bz", 4)
        else:
            arrived("bz", distance, way)
        dz = from_way(way, distance)
        where = column(dz, RA, RB)
        send(("ap",), where, where, partner)

    def agend():
        arrived("ap")
        gathered[4, 0, 0] = gathered[0, 0, 0]

    def build(target, dz, owner, added=None):
        shift = corners[0] % PLANES

        def one(dx, carry):
            block = ((x + dx) % NXC) * 16 + ((z + dz) % NZC) * 2 + owner
            after = table[block] - shift
            before = table[(block + 63) % 64] + PLANES - shift
            for at in range(0, PLANES, 2):
                planes = [
                    terms[plane + jnp.where(plane >= shift, after, before)]
                    for plane in (at, at + 1)
                ]
                value = jnp.concatenate(planes, axis=0)
                rows = pl.ds(at * 8, TILE)
                if added is not None:
                    value = value + added[dz, dx, rows, :].astype(f32)
                target[dz, dx, rows, :] = value.astype(bf16)
            return carry

        lax.fori_loop(0, NXC, one, 0)

    def bpart(dz):
        build(part_out, dz, 1 - core)
        send(("part", dz), part_out.at[dz], part_in.at[dz], partner)

    def bown(dz):
        arrived("part", dz)
        build(sums, dz, core, part_in)

    def add(where, start, size, *others):
        total = where[pl.ds(start, size), :].astype(f32)
        for other in others:
            total = total + other[...].astype(f32)
        where[pl.ds(start, size), :] = total.astype(bf16)

    def rax1(dz):
        for way in range(2):
            part = sums.at[dz, 2, pl.ds(way * HA, HA)]
            send(("rax1", dz, way), part, xa1.at[dz, way], along_x[way])

    def rax2(dz, way):
        dx = 1 if way == 0 else 3
        arrived("rax1", dz, way)
        add(sums.at[dz, dx], way * HA, HA, xa1.at[dz, way])
        part = sums.at[dz, dx, pl.ds(0, RA)]
        send(("rax2", dz), part, xa2.at[dz, way], along_x[way])

    def rax3(dz):
        arrived("rax2", dz)
        add(sums.at[dz, 0], 0, RA, xa2.at[dz, 0], xa2.at[dz, 1])

    def raz(step, way=None):
        if step == 1:
            for way in range(2):
                part = sums.at[4, 0, pl.ds(way * HA, HA)]
                send(("raz", 1, way), part, za1.at[way], along_z[way])
            return
        dz = 5 - step if way == 0 else 3 + step
        arrived("raz", step - 1, way)
        if step == 2:
            add(sums.at[dz, 0], way * HA, HA, za1.at[way])
        else:
            add(sums.at[dz, 0], 0, RA, za.at[step - 3, way])
        part = sums.at[dz, 0, pl.ds(0, RA)]
        send(("raz", 4) if step == 4 else ("raz", step, way), part, za.at[step - 2, way], along_z[way])

    def rbz(dx, step, way=None):
        if step == 1:
            for way in range(2):
                part = sums.at[4, dx, pl.ds(RA + way * HB, HB)]
                send(("rbz", dx, 1, way), part, zb1.at[way, dx], along_z[way])
            return
        dz = 5 - step if way == 0 else 3 + step
        arrived("rbz", dx, step - 1, way)
        if step == 2:
            add(sums.at[dz, dx], RA + way * HB, HB, zb1.at[way, dx])
        else:
            add(sums.at[dz, dx], RA, RB, zb.at[step - 3, way, dx])
        part = sums.at[dz, dx, pl.ds(RA, RB)]
        send(("rbz", dx, 4) if step == 4 else ("rbz", dx, step, way), part, zb.at[step - 2, way, dx], along_z[way])

    def rbz_end(dx):
        arrived("rbz", dx, 4)
        add(sums.at[0, dx], RA, RB, zb.at[2, 0, dx], zb.at[2, 1, dx])

    def rbx1():
        rbz_end(2)
        for way in range(2):
            part = sums.at[0, 2, pl.ds(RA + way * HB, HB)]
            send(("rbx1", way), part, xb1.at[way], along_x[way])

    def rbx2(way):
        dx = 1 if way == 0 else 3
        rbz_end(dx)
        arrived("rbx1", way)
        add(sums.at[0, dx], RA + way * HB, HB, xb1.at[way])
        send(("rbx2",), sums.at[0, dx, pl.ds(RA, RB)], xb2.at[way], along_x[way])

    def rsend():
        arrived("raz", 4)
        arrived("rbz", 0, 4)
        arrived("rbx2")
        dens[pl.ds(0, RA), :] = (
            sums[0, 0, pl.ds(0, RA), :].astype(f32)
            + za[2, 0].astype(f32) + za[2, 1].astype(f32)
        )
        dens[pl.ds(RA, RB), :] = (
            sums[0, 0, pl.ds(RA, RB), :].astype(f32)
            + zb[2, 0, 0].astype(f32) + zb[2, 1, 0].astype(f32)
            + xb2[0].astype(f32) + xb2[1].astype(f32)
        )
        loads["density"] = pltpu.make_async_copy(dens, density, out_sem.at[PAIRS])
        loads["density"].start()

    def halo():
        for pair in range(PAIRS):
            where = pl.ds(2 * pair, 2)
            send(("halo", pair), support.at[where], left.at[where], y_next)
            send(("halo", pair), support.at[where], right.at[where], y_prev)

    def lap(pair):
        if pair == first_lap:
            loads["mixes"].wait()
        arrived("halo", pair)
        first = 2 * pair
        cells = jnp.concatenate([
            jnp.concatenate([ref[first], ref[first + 1]], axis=1) for ref in (own, left, right)
        ], axis=0)
        high, low = (
            jnp.concatenate([mixes[at + piece] for piece in range(6)], axis=1) for at in (0, 6)
        )
        total = jnp.dot(high, cells, preferred_element_type=f32)
        total = total + jnp.dot(low, cells, preferred_element_type=f32)
        for index in range(2):
            values = own[first + index]
            twice = jnp.concatenate([values, values], axis=1)
            kinetic[first + index] = total[:, index * LANES:(index + 1) * LANES] + jnp.dot(
                twice, mixes[12], preferred_element_type=f32
            )

    def fin(pair):
        first = 2 * pair
        flat = gathered.reshape(5 * NZC * 2 * TILES, TILE, LANES)
        for func in (first, first + 1):
            corner = corners[func]
            window = flat[pl.ds(corner // 2, TILES + 1)].astype(f32).reshape(ROWS + TILE, LANES)
            local = jnp.where(corner % 2 == 1, window[8:8 + ROWS], window[:ROWS])
            term = (local * own[func].astype(f32)).astype(bf16).astype(f32)
            out[func] = (kinetic[func] + term).astype(bf16)
        loads["out", pair] = pltpu.make_async_copy(
            out.at[pl.ds(first, 2)], applied.at[pl.ds(first, 2)], out_sem.at[pair]
        )
        loads["out", pair].start()

    loads["corners"].wait()
    bases = [corners[k] // 32 for k in range(FUNCS)]

    def find(block, carry):
        found = FUNCS
        for k in reversed(range(FUNCS)):
            found = jnp.where(bases[k] == block, k, found)
        table[block] = found * PLANES
        return carry

    lax.fori_loop(0, 64, find, 0)
    terms[pl.ds(FUNCS * PLANES, PLANES)] = jnp.zeros((PLANES, 8, LANES), f32)
    loads["potential"].wait()
    gathered[x, z, core] = pot_in[...].astype(bf16).reshape(TILES, TILE, LANES)
    loads["occupation"].wait()
    loads["support"].wait()
    spread = jnp.broadcast_to(occupation[...].astype(f32).reshape(1, FUNCS), (FUNCS, FUNCS))
    lane = lax.broadcasted_iota(jnp.int32, (FUNCS, FUNCS), 1)
    diagonal = lane == lax.broadcasted_iota(jnp.int32, (FUNCS, FUNCS), 0)
    column_weights = jnp.sum(jnp.where(diagonal, spread, 0.0), axis=1, keepdims=True)
    for k in range(FUNCS):
        weights[k] = jnp.broadcast_to(column_weights[k:k + 1], (8, LANES))
    weights[FUNCS] = jnp.zeros((8, LANES), f32)

    for k in range(FUNCS):
        value = own[k].astype(f32).reshape(PLANES, 8, LANES)
        total = weights[k] * value * value
        if k + 1 < FUNCS:
            twin = FUNCS
            for other in reversed(range(k + 1, FUNCS)):
                twin = jnp.where(bases[other] == bases[k], other, twin)
            second = own[jnp.minimum(twin, FUNCS - 1)].astype(f32).reshape(PLANES, 8, LANES)
            total = total + weights[twin] * second * second
        terms[pl.ds(k * PLANES, PLANES)] = total
    pl.semaphore_wait(barrier, len(neighbours))

    steps = {step.__name__: step for step in (
        az, ax1, ax2, ap, bx1, bx2, bz, bp, agend, bpart, bown, rax1, rax2, rax3,
        raz, rbz, rbx1, rbx2, rsend, halo, lap, fin,
    )}
    first_lap = next(args[0] for name, *args in ORDER if name == "lap")
    for name, *args in ORDER:
        steps[name](*args)
    assert sum(rows) == SENT_ROWS, sum(rows)
    pltpu.make_async_copy(tally, tally, send_sem).wait()
    for pair in range(PAIRS):
        loads["out", pair].wait()
    loads["density"].wait()


def store(applied, density, applied_out, density_out, sems):
    copies = [
        pltpu.make_async_copy(applied, applied_out, sems.at[0]),
        pltpu.make_async_copy(density, density_out, sems.at[1]),
    ]
    for copy in copies:
        copy.start()
    for copy in copies:
        copy.wait()


def on_device(support, corners, occupation, potential):
    mixes = stencil_matrices()
    bf16, f32 = jnp.bfloat16, jnp.float32
    vmem = lambda shape, kind=bf16: pltpu.VMEM(shape, kind)
    in_hbm = lambda array: pltpu.with_memory_space_constraint(array, pltpu.HBM)
    anywhere = pl.BlockSpec(memory_space=pl.ANY)
    copies = 122
    applied, density = pl.pallas_call(
        kernel,
        out_shape=(
            jax.ShapeDtypeStruct((FUNCS, ROWS, LANES), bf16),
            jax.ShapeDtypeStruct((ROWS, LANES), f32),
        ),
        in_specs=[anywhere] * 5,
        out_specs=(anywhere, anywhere),
        scratch_shapes=[
            pltpu.SMEM((FUNCS,), jnp.int32),
            vmem((FUNCS,)),
            vmem((FUNCS + 1, 8, LANES), f32),
            vmem((FUNCS, ROWS, LANES)),
            vmem((FUNCS, ROWS, LANES)),
            vmem((FUNCS, ROWS, LANES)),
            vmem((FUNCS, ROWS, LANES)),
            vmem((ROWS, LANES), f32),
            vmem((ROWS, LANES), f32),
            vmem((len(mixes), ROWS, LANES)),
            vmem((FUNCS, ROWS, LANES), f32),
            vmem((NXC + 1, NZC, 2, TILES, TILE, LANES)),
            vmem(((FUNCS + 1) * PLANES, 8, LANES), f32),
            pltpu.SMEM((64,), jnp.int32),
            vmem((NZC, NXC, ROWS, LANES)),
            vmem((NZC, NXC, ROWS, LANES)),
            vmem((NZC, NXC, ROWS, LANES)),
            vmem((NZC, 2, HA, LANES)),
            vmem((NZC, 2, RA, LANES)),
            vmem((2, HA, LANES)),
            vmem((3, 2, RA, LANES)),
            vmem((2, NXC, HB, LANES)),
            vmem((3, 2, NXC, RB, LANES)),
            vmem((2, HB, LANES)),
            vmem((2, RB, LANES)),
            vmem((SENT_ROWS, LANES)),
            pltpu.SemaphoreType.DMA((5,)),
            pltpu.SemaphoreType.DMA((PAIRS + 1,)),
            pltpu.SemaphoreType.DMA,
            pltpu.SemaphoreType.DMA((copies,)),
        ],
        compiler_params=pltpu.CompilerParams(
            collective_id=0, has_side_effects=True, vmem_limit_bytes=48 * 1024 * 1024
        ),
    )(
        in_hbm(corners),
        in_hbm(occupation),
        in_hbm(support.reshape(FUNCS, ROWS, LANES)),
        in_hbm(potential.reshape(ROWS, LANES)),
        in_hbm(jnp.asarray(mixes)),
    )
    applied, density = pl.pallas_call(
        store,
        out_shape=(
            jax.ShapeDtypeStruct((FUNCS, ROWS, LANES), bf16),
            jax.ShapeDtypeStruct((ROWS, LANES), f32),
        ),
        in_specs=[anywhere] * 2,
        out_specs=(anywhere, anywhere),
        scratch_shapes=[pltpu.SemaphoreType.DMA((2,))],
        compiler_params=pltpu.CompilerParams(vmem_limit_bytes=8 * 1024 * 1024),
    )(applied, density)
    return applied.reshape(support.shape), density.reshape(potential.shape)


def solution(mesh):
    in_specs = (P("grp", None, "slab", None), P("grp"), P("grp"), P("grp", "slab", None))
    out_specs = (P("grp", None, "slab", None), P("grp", "slab", None))
    return jax.shard_map(
        on_device, mesh=mesh, in_specs=in_specs, out_specs=out_specs, check_vma=False
    )
```

```python
import functools
import math

import jax
import jax.numpy as jnp
import numpy as np
from jax import lax
from jax.experimental import pallas as pl
from jax.experimental.pallas import tpu as pltpu
from jax.sharding import PartitionSpec as P

MESH = pl.DeviceIdType.MESH
FUNCS, ROWS, LANES = 16, 256, 128
NXC, NZC = 4, 8
PAIRS = FUNCS // 2
TILE = 16
PLANES, TILES = ROWS // 8, ROWS // TILE
RA = 160
RB = ROWS - RA
HA, HB = RA // 2, RB // 2
SENT_ROWS = 40448

kinetic_taps = [
    2.0 * (-1.0) ** (index + 2) / float((index + 1) * (index + 1)) for index in range(8)
]
center_tap = -math.pi * math.pi / 3.0


ORDER = (
    ("az", 1, 1), ("bx1",), ("az", 1, 0), ("bpart", 4), ("ax1", 0), ("bpart", 5), ("halo",), ("bpart", 3),
    ("bown", 4), ("rax1", 4), ("rbz", 1, 1), ("bown", 5), ("rax1", 5), ("rbz", 2, 1), ("bx2", 0), ("bx2", 1),
    ("ax1", 1), ("az", 2, 0), ("az", 2, 1), ("bown", 3), ("rax1", 3), ("rbz", 0, 1), ("bpart", 6), ("ax1", 7),
    ("ax2", 0, 1), ("bpart", 2), ("rbz", 3, 1), ("rbz", 1, 2, 0), ("rbz", 1, 2, 1), ("rax2", 4, 0),
    ("rax2", 4, 1), ("rbz", 2, 2, 1), ("rbz", 2, 2, 0), ("bz", 1, 1), ("bz", 1, 0), ("ax2", 0, 0),
    ("bown", 2), ("rax1", 2), ("bown", 6), ("rax1", 6), ("rax2", 5, 1), ("az", 3, 0), ("rax2", 5, 0),
    ("bpart", 7), ("rbz", 3, 2, 0), ("rbz", 3, 2, 1), ("rax2", 3, 1), ("rax2", 3, 0), ("az", 3, 1),
    ("ax1", 6), ("rbz", 2, 3, 0), ("ax1", 2), ("rbz", 0, 2, 1), ("rax3", 4), ("raz", 1), ("bown", 7),
    ("bpart", 1), ("rbz", 2, 3, 1), ("rbz", 0, 2, 0), ("rax2", 6, 1), ("rax1", 7), ("rax2", 6, 0),
    ("rax2", 2, 0), ("bz", 2, 1), ("bz", 2, 0), ("rbz", 1, 3, 1), ("rax3", 5), ("bpart", 0), ("ax2", 1, 1),
    ("ax2", 7, 1), ("az", 4, 0), ("ax2", 1, 0), ("az", 4, 1), ("bown", 1), ("rax2", 2, 1), ("rbz", 1, 3, 0),
    ("rbz", 3, 3, 1), ("bown", 0), ("rax1", 0), ("rax1", 1), ("rbz", 2, 4, 0), ("rbz", 3, 3, 0),
    ("rbz", 2, 4, 1), ("ax2", 7, 0), ("ap", 0), ("raz", 2, 1), ("ax2", 6, 1), ("ax2", 2, 1), ("ax1", 5),
    ("ax2", 2, 0), ("rax3", 3), ("raz", 2, 0), ("ax1", 3), ("bz", 3, 1), ("bz", 3, 0), ("rax3", 6),
    ("bp", 1, 1), ("lap", 2), ("ax1", 4), ("bp", 2, 1), ("rax2", 7, 1), ("ax2", 6, 0), ("lap", 0),
    ("rbz", 0, 3, 1), ("rax2", 1, 1), ("rbz", 0, 3, 0), ("rbz", 3, 4, 1), ("rax2", 7, 0), ("lap", 3),
    ("rbz", 1, 4, 0), ("ap", 1), ("raz", 3, 1), ("rax2", 1, 0), ("rax3", 2), ("raz", 3, 0), ("rbx1",),
    ("rbz", 3, 4, 0), ("ax2", 5, 1), ("rbz", 1, 4, 1), ("ax2", 5, 0), ("ax2", 3, 0), ("ap", 7), ("ax2", 3, 1),
    ("bz", 4, 1), ("bz", 4, 0), ("ax2", 4, 0), ("bp", 1, 0), ("ax2", 4, 1), ("rax2", 0, 1), ("rax2", 0, 0),
    ("bp", 0), ("rbz", 0, 4, 1), ("lap", 5), ("bp", 3, 0), ("rbz", 0, 4, 0), ("ap", 2), ("ap", 6),
    ("rax3", 7), ("bp", 3, 1), ("bp", 2, 0), ("raz", 4, 1), ("rax3", 1), ("raz", 4, 0), ("rbx2", 0),
    ("rbx2", 1), ("ap", 5), ("ap", 3), ("lap", 1), ("ap", 4), ("bp", 4), ("lap", 4), ("lap", 6), ("rax3", 0),
    ("lap", 7), ("agend",), ("fin", 1), ("fin", 5), ("fin", 0), ("fin", 4), ("fin", 3), ("fin", 2),
    ("fin", 6), ("fin", 7), ("rsend",),
)


def split_bf16(matrix):
    high = matrix.astype(jnp.bfloat16)
    low = (matrix - high.astype(np.float64)).astype(jnp.bfloat16)
    return high, low


def stencil_matrices():
    along_y, along_x = np.zeros((32, 32)), np.zeros((8, 8))
    left, right, along_z = np.zeros((8, 8)), np.zeros((8, 8)), np.zeros((LANES, LANES))
    for offset in range(1, 9):
        weight = kinetic_taps[offset - 1]
        along_y += weight * (np.eye(32, k=offset) + np.eye(32, k=-offset))
        along_x += weight * (np.eye(8, k=offset) + np.eye(8, k=-offset))
        left += weight * np.eye(8, k=8 - offset)
        right += weight * np.eye(8, k=offset - 8)
        along_z += weight * (
            np.roll(np.eye(LANES), offset, 1) + np.roll(np.eye(LANES), -offset, 1)
        )
    own = (
        np.kron(along_y, np.eye(8))
        + np.kron(np.eye(32), along_x)
        + 3.0 * center_tap * np.eye(ROWS)
    )
    rows = np.concatenate(
        [own, np.kron(np.eye(32), left), np.kron(np.eye(32), right)], axis=1
    )
    rows_high, rows_low = split_bf16(-0.5 * rows)
    z_high, z_low = split_bf16(-0.5 * along_z)
    halves = [part[:, at:at + LANES] for part in (rows_high, rows_low) for at in range(0, 3 * ROWS, LANES)]
    mixes = np.stack([*halves, np.concatenate([z_high, z_low], axis=0)])
    return mixes.reshape(len(mixes), PLANES, 8, LANES)


def kernel(
    corners_in, occupation_in, support, potential, mixes_in,
    applied, density,
    corners, occupation, weights, own, left, right, pot_in, mixes,
    kinetic, gathered, terms, table, part_out, part_in, sums,
    xa1, xa2, za1, za, zb1, zb, xb1, xb2, tally,
    load_sem, send_sem, recv_sem,
):
    f32, bf16 = jnp.float32, jnp.bfloat16
    group, slab = lax.axis_index("grp"), lax.axis_index("slab")
    x, z, core = group // 16, (group // 2) % 8, group % 2

    def chip(dx, dz):
        return ((((x + dx) % NXC) * NZC + (z + dz) % NZC) * 2 + core, slab)

    partner = (group + 1 - 2 * core, slab)
    x_next, x_prev = chip(1, 0), chip(NXC - 1, 0)
    z_next, z_prev = chip(0, 1), chip(0, NZC - 1)
    y_next, y_prev = (group, (slab + 1) % 4), (group, (slab + 3) % 4)
    along_x, along_z, along_y = (x_next, x_prev), (z_next, z_prev), (y_next, y_prev)

    loads = {}
    for index, (name, src, dst) in enumerate([
        ("corners", corners_in, corners),
        ("potential", potential, pot_in),
        ("occupation", occupation_in, occupation),
        ("support", support, own),
        ("mixes", mixes_in.reshape(mixes.shape), mixes),
    ]):
        loads[name] = pltpu.make_async_copy(src, dst, load_sem.at[index])
        loads[name].start()

    slots, pending, rows = {}, {}, []

    def send(name, src, dst, device):
        index = slots.setdefault(name, len(slots))
        rows.append(math.prod(src.shape[:-1]))
        pending[name] = pending.get(name, 0) + rows[-1]
        pltpu.make_async_remote_copy(
            src_ref=src, dst_ref=dst,
            send_sem=send_sem, recv_sem=recv_sem.at[index],
            device_id=device, device_id_type=MESH,
        ).start()

    barrier = pltpu.get_barrier_semaphore()
    neighbours = (*along_x, *along_z, *along_y, partner)
    for device in neighbours:
        pl.semaphore_signal(barrier, inc=1, device_id=device, device_id_type=MESH)

    def arrived(*name):
        if name in pending:
            whole = tally.at[pl.ds(0, pending.pop(name))]
            pltpu.make_async_copy(whole, whole, recv_sem.at[slots[name]]).wait()

    def slot(dx, dz, start, size):
        tiles = pl.ds(start // TILE, size // TILE)
        return gathered.at[(x + dx) % NXC, (z + dz) % NZC, core, tiles]

    def column(dz, start, size):
        tiles = pl.ds(start // TILE, size // TILE)
        return gathered.at[pl.ds(0, NXC), (z + dz) % NZC, core, tiles]

    def from_way(way, distance):
        return (NZC - distance) % NZC if way == 0 else distance

    def az(step, way):
        if step > 1:
            arrived("az", step - 1, way)
        dz = from_way(way, step - 1)
        where = slot(0, dz, 0, RA) if step < 4 else slot(0, dz, way * HA, HA)
        send(("az", 4) if step == 4 else ("az", step, way), where, where, along_z[way])

    def ax1(dz):
        if dz == 4:
            arrived("az", 4)
        elif dz:
            arrived("az", min(dz, NZC - dz), 0 if dz > 4 else 1)
        for way in range(2):
            where = slot(0, dz, 0, RA)
            send(("ax1", dz, way), where, where, along_x[way])

    def ax2(dz, way):
        arrived("ax1", dz, way)
        where = slot(3 if way == 0 else 1, dz, way * HA, HA)
        send(("ax2", dz), where, where, along_x[way])

    def ap(dz):
        arrived("ax2", dz)
        where = column(dz, 0, RA)
        send(("ap",), where, where, partner)

    def bx1():
        for way in range(2):
            where = slot(0, 0, RA, RB)
            send(("bx1", way), where, where, along_x[way])

    def bx2(way):
        arrived("bx1", way)
        where = slot(3 if way == 0 else 1, 0, RA + way * HB, HB)
        send(("bx2",), where, where, along_x[way])

    def bz(step, way):
        if step == 1:
            arrived("bx2")
        else:
            arrived("bz", step - 1, way)
        dz = from_way(way, step - 1)
        where = column(dz, RA, RB) if step < 4 else column(dz, RA + way * HB, HB)
        send(("bz", 4) if step == 4 else ("bz", step, way), where, where, along_z[way])

    def bp(distance, way=0):
        if distance == 0:
            arrived("bx2")
        elif distance == 4:
            arrived("bz", 4)
        else:
            arrived("bz", distance, way)
        dz = from_way(way, distance)
        where = column(dz, RA, RB)
        send(("ap",), where, where, partner)

    def agend():
        arrived("ap")
        gathered[4, 0, 0] = gathered[0, 0, 0]

    def build(target, dz, owner, added=None):
        shift = corners[0] % PLANES

        def one(dx, carry):
            block = ((x + dx) % NXC) * 16 + ((z + dz) % NZC) * 2 + owner
            after = table[block] - shift
            before = table[(block + 63) % 64] + PLANES - shift
            for at in range(0, PLANES, 2):
                planes = [
                    terms[plane + jnp.where(plane >= shift, after, before)]
                    for plane in (at, at + 1)
                ]
                value = jnp.concatenate(planes, axis=0)
                rows = pl.ds(at * 8, TILE)
                if added is not None:
                    value = value + added[dz, dx, rows, :].astype(f32)
                target[dz, dx, rows, :] = value.astype(bf16)
            return carry

        lax.fori_loop(0, NXC, one, 0)

    def bpart(dz):
        build(part_out, dz, 1 - core)
        send(("part", dz), part_out.at[dz], part_in.at[dz], partner)

    def bown(dz):
        arrived("part", dz)
        build(sums, dz, core, part_in)

    def add(where, start, size, *others):
        total = where[pl.ds(start, size), :].astype(f32)
        for other in others:
            total = total + other[...].astype(f32)
        where[pl.ds(start, size), :] = total.astype(bf16)

    def rax1(dz):
        for way in range(2):
            part = sums.at[dz, 2, pl.ds(way * HA, HA)]
            send(("rax1", dz, way), part, xa1.at[dz, way], along_x[way])

    def rax2(dz, way):
        dx = 1 if way == 0 else 3
        arrived("rax1", dz, way)
        add(sums.at[dz, dx], way * HA, HA, xa1.at[dz, way])
        part = sums.at[dz, dx, pl.ds(0, RA)]
        send(("rax2", dz), part, xa2.at[dz, way], along_x[way])

    def rax3(dz):
        arrived("rax2", dz)
        add(sums.at[dz, 0], 0, RA, xa2.at[dz, 0], xa2.at[dz, 1])

    def raz(step, way=None):
        if step == 1:
            for way in range(2):
                part = sums.at[4, 0, pl.ds(way * HA, HA)]
                send(("raz", 1, way), part, za1.at[way], along_z[way])
            return
        dz = 5 - step if way == 0 else 3 + step
        arrived("raz", step - 1, way)
        if step == 2:
            add(sums.at[dz, 0], way * HA, HA, za1.at[way])
        else:
            add(sums.at[dz, 0], 0, RA, za.at[step - 3, way])
        part = sums.at[dz, 0, pl.ds(0, RA)]
        send(("raz", 4) if step == 4 else ("raz", step, way), part, za.at[step - 2, way], along_z[way])

    def rbz(dx, step, way=None):
        if step == 1:
            for way in range(2):
                part = sums.at[4, dx, pl.ds(RA + way * HB, HB)]
                send(("rbz", dx, 1, way), part, zb1.at[way, dx], along_z[way])
            return
        dz = 5 - step if way == 0 else 3 + step
        arrived("rbz", dx, step - 1, way)
        if step == 2:
            add(sums.at[dz, dx], RA + way * HB, HB, zb1.at[way, dx])
        else:
            add(sums.at[dz, dx], RA, RB, zb.at[step - 3, way, dx])
        part = sums.at[dz, dx, pl.ds(RA, RB)]
        send(("rbz", dx, 4) if step == 4 else ("rbz", dx, step, way), part, zb.at[step - 2, way, dx], along_z[way])

    def rbz_end(dx):
        arrived("rbz", dx, 4)
        add(sums.at[0, dx], RA, RB, zb.at[2, 0, dx], zb.at[2, 1, dx])

    def rbx1():
        rbz_end(2)
        for way in range(2):
            part = sums.at[0, 2, pl.ds(RA + way * HB, HB)]
            send(("rbx1", way), part, xb1.at[way], along_x[way])

    def rbx2(way):
        dx = 1 if way == 0 else 3
        rbz_end(dx)
        arrived("rbx1", way)
        add(sums.at[0, dx], RA + way * HB, HB, xb1.at[way])
        send(("rbx2",), sums.at[0, dx, pl.ds(RA, RB)], xb2.at[way], along_x[way])

    def rsend():
        arrived("raz", 4)
        arrived("rbz", 0, 4)
        arrived("rbx2")
        density[pl.ds(0, RA), :] = (
            sums[0, 0, pl.ds(0, RA), :].astype(f32)
            + za[2, 0].astype(f32) + za[2, 1].astype(f32)
        )
        density[pl.ds(RA, RB), :] = (
            sums[0, 0, pl.ds(RA, RB), :].astype(f32)
            + zb[2, 0, 0].astype(f32) + zb[2, 1, 0].astype(f32)
            + xb2[0].astype(f32) + xb2[1].astype(f32)
        )

    def halo():
        for pair in range(PAIRS):
            where = pl.ds(2 * pair, 2)
            send(("halo", pair), support.at[where], left.at[where], y_next)
            send(("halo", pair), support.at[where], right.at[where], y_prev)

    def lap(pair):
        if pair == first_lap:
            loads["mixes"].wait()
        arrived("halo", pair)
        first = 2 * pair
        cells = jnp.concatenate([
            jnp.concatenate([ref[first], ref[first + 1]], axis=1) for ref in (own, left, right)
        ], axis=0)
        high, low = (
            jnp.concatenate([mixes[at + piece] for piece in range(6)], axis=1) for at in (0, 6)
        )
        total = jnp.dot(high, cells, preferred_element_type=f32)
        total = total + jnp.dot(low, cells, preferred_element_type=f32)
        for index in range(2):
            values = own[first + index]
            twice = jnp.concatenate([values, values], axis=1)
            kinetic[first + index] = total[:, index * LANES:(index + 1) * LANES] + jnp.dot(
                twice, mixes[12], preferred_element_type=f32
            )

    def fin(pair):
        first = 2 * pair
        flat = gathered.reshape(5 * NZC * 2 * TILES, TILE, LANES)
        for func in (first, first + 1):
            corner = corners[func]
            window = flat[pl.ds(corner // 2, TILES + 1)].astype(f32).reshape(ROWS + TILE, LANES)
            local = jnp.where(corner % 2 == 1, window[8:8 + ROWS], window[:ROWS])
            term = (local * own[func].astype(f32)).astype(bf16).astype(f32)
            applied[func] = (kinetic[func] + term).astype(bf16)

    loads["corners"].wait()
    bases = [corners[k] // 32 for k in range(FUNCS)]

    def find(block, carry):
        found = FUNCS
        for k in reversed(range(FUNCS)):
            found = jnp.where(bases[k] == block, k, found)
        table[block] = found * PLANES
        return carry

    lax.fori_loop(0, 64, find, 0)
    terms[pl.ds(FUNCS * PLANES, PLANES)] = jnp.zeros((PLANES, 8, LANES), f32)
    loads["potential"].wait()
    gathered[x, z, core] = pot_in[...].astype(bf16).reshape(TILES, TILE, LANES)
    loads["occupation"].wait()
    loads["support"].wait()
    spread = jnp.broadcast_to(occupation[...].astype(f32).reshape(1, FUNCS), (FUNCS, FUNCS))
    lane = lax.broadcasted_iota(jnp.int32, (FUNCS, FUNCS), 1)
    diagonal = lane == lax.broadcasted_iota(jnp.int32, (FUNCS, FUNCS), 0)
    column_weights = jnp.sum(jnp.where(diagonal, spread, 0.0), axis=1, keepdims=True)
    for k in range(FUNCS):
        weights[k] = jnp.broadcast_to(column_weights[k:k + 1], (8, LANES))
    weights[FUNCS] = jnp.zeros((8, LANES), f32)

    for k in range(FUNCS):
        value = own[k].astype(f32).reshape(PLANES, 8, LANES)
        total = weights[k] * value * value
        if k + 1 < FUNCS:
            twin = FUNCS
            for other in reversed(range(k + 1, FUNCS)):
                twin = jnp.where(bases[other] == bases[k], other, twin)
            second = own[jnp.minimum(twin, FUNCS - 1)].astype(f32).reshape(PLANES, 8, LANES)
            total = total + weights[twin] * second * second
        terms[pl.ds(k * PLANES, PLANES)] = total
    pl.semaphore_wait(barrier, len(neighbours))

    steps = {step.__name__: step for step in (
        az, ax1, ax2, ap, bx1, bx2, bz, bp, agend, bpart, bown, rax1, rax2, rax3,
        raz, rbz, rbx1, rbx2, rsend, halo, lap, fin,
    )}
    first_lap = next(args[0] for name, *args in ORDER if name == "lap")
    for name, *args in ORDER:
        steps[name](*args)
    assert sum(rows) == SENT_ROWS, sum(rows)
    pltpu.make_async_copy(tally, tally, send_sem).wait()


def store(applied, density, applied_out, density_out, sems):
    copies = [
        pltpu.make_async_copy(applied, applied_out, sems.at[0]),
        pltpu.make_async_copy(density, density_out, sems.at[1]),
    ]
    for copy in copies:
        copy.start()
    for copy in copies:
        copy.wait()


def on_device(support, corners, occupation, potential):
    mixes = stencil_matrices()
    bf16, f32 = jnp.bfloat16, jnp.float32
    vmem = lambda shape, kind=bf16: pltpu.VMEM(shape, kind)
    in_hbm = lambda array: pltpu.with_memory_space_constraint(array, pltpu.HBM)
    anywhere = pl.BlockSpec(memory_space=pl.ANY)
    in_vmem = pl.BlockSpec(memory_space=pltpu.VMEM)
    copies = 122
    applied, density = pl.pallas_call(
        kernel,
        out_shape=(
            pltpu.VMEM((FUNCS, ROWS, LANES), bf16),
            pltpu.VMEM((ROWS, LANES), f32),
        ),
        in_specs=[anywhere] * 5,
        out_specs=(in_vmem, in_vmem),
        scratch_shapes=[
            pltpu.SMEM((FUNCS,), jnp.int32),
            vmem((FUNCS,)),
            vmem((FUNCS + 1, 8, LANES), f32),
            vmem((FUNCS, ROWS, LANES)),
            vmem((FUNCS, ROWS, LANES)),
            vmem((FUNCS, ROWS, LANES)),
            vmem((ROWS, LANES), f32),
            vmem((len(mixes), ROWS, LANES)),
            vmem((FUNCS, ROWS, LANES), f32),
            vmem((NXC + 1, NZC, 2, TILES, TILE, LANES)),
            vmem(((FUNCS + 1) * PLANES, 8, LANES), f32),
            pltpu.SMEM((64,), jnp.int32),
            vmem((NZC, NXC, ROWS, LANES)),
            vmem((NZC, NXC, ROWS, LANES)),
            vmem((NZC, NXC, ROWS, LANES)),
            vmem((NZC, 2, HA, LANES)),
            vmem((NZC, 2, RA, LANES)),
            vmem((2, HA, LANES)),
            vmem((3, 2, RA, LANES)),
            vmem((2, NXC, HB, LANES)),
            vmem((3, 2, NXC, RB, LANES)),
            vmem((2, HB, LANES)),
            vmem((2, RB, LANES)),
            vmem((SENT_ROWS, LANES)),
            pltpu.SemaphoreType.DMA((5,)),
            pltpu.SemaphoreType.DMA,
            pltpu.SemaphoreType.DMA((copies,)),
        ],
        compiler_params=pltpu.CompilerParams(
            collective_id=0, has_side_effects=True, vmem_limit_bytes=48 * 1024 * 1024
        ),
    )(
        in_hbm(corners),
        in_hbm(occupation),
        in_hbm(support.reshape(FUNCS, ROWS, LANES)),
        in_hbm(potential.reshape(ROWS, LANES)),
        in_hbm(jnp.asarray(mixes)),
    )
    applied, density = pl.pallas_call(
        store,
        out_shape=(
            jax.ShapeDtypeStruct((FUNCS, ROWS, LANES), bf16),
            jax.ShapeDtypeStruct((ROWS, LANES), f32),
        ),
        in_specs=[anywhere] * 2,
        out_specs=(anywhere, anywhere),
        scratch_shapes=[pltpu.SemaphoreType.DMA((2,))],
        compiler_params=pltpu.CompilerParams(vmem_limit_bytes=8 * 1024 * 1024),
    )(applied, density)
    return applied.reshape(support.shape), density.reshape(potential.shape)


def solution(mesh):
    in_specs = (P("grp", None, "slab", None), P("grp"), P("grp"), P("grp", "slab", None))
    out_specs = (P("grp", None, "slab", None), P("grp", "slab", None))
    return jax.shard_map(
        on_device, mesh=mesh, in_specs=in_specs, out_specs=out_specs, check_vma=False
    )
```

```python
import functools
import math

import jax
import jax.numpy as jnp
import numpy as np
from jax import lax
from jax.experimental import pallas as pl
from jax.experimental.pallas import tpu as pltpu
from jax.sharding import PartitionSpec as P

MESH = pl.DeviceIdType.MESH
FUNCS, ROWS, LANES = 16, 256, 128
NXC, NZC = 4, 8
PAIRS = FUNCS // 2
TILE = 16
PLANES, TILES = ROWS // 8, ROWS // TILE
GA, SA = 144, 160
GB, SB = ROWS - GA, ROWS - SA
SENT_ROWS = 40448

kinetic_taps = [
    2.0 * (-1.0) ** (index + 2) / float((index + 1) * (index + 1)) for index in range(8)
]
center_tap = -math.pi * math.pi / 3.0


ORDER = (
    ("bx1",), ("az", 1, 1), ("bpart", 4), ("az", 1, 0), ("bpart", 3), ("halo",), ("bpart", 5), ("ax1", 0),
    ("bz", 0, 1, 1), ("bz", 0, 1, 0), ("bown", 4), ("rbz", 3, 1), ("rax1", 4), ("rbz", 2, 1), ("bpart", 6),
    ("rbz", 0, 1), ("bown", 3), ("rax1", 3), ("rbz", 1, 1), ("bown", 5), ("rax1", 5), ("bz", 3, 1, 0),
    ("bz", 3, 1, 1), ("bx2", 1), ("bz", 1, 1, 0), ("bz", 1, 1, 1), ("bx2", 0), ("ax1", 1), ("bown", 6),
    ("bpart", 7), ("bpart", 1), ("az", 2, 1), ("az", 2, 0), ("ax1", 7), ("rax1", 6), ("bpart", 2),
    ("bz", 0, 2, 0), ("bz", 0, 2, 1), ("rbz", 2, 2, 0), ("rax2", 4, 1), ("rbz", 2, 2, 1), ("rax2", 4, 0),
    ("rbz", 1, 2, 0), ("rax2", 3, 0), ("ax2", 0, 0), ("rbz", 3, 2, 1), ("rbz", 3, 2, 0), ("bown", 2),
    ("rax1", 2), ("bz", 3, 2, 1), ("bz", 3, 2, 0), ("rax2", 3, 1), ("bz", 2, 1, 1), ("rax2", 5, 1),
    ("ax2", 0, 1), ("bz", 2, 1, 0), ("az", 3, 0), ("rbz", 1, 2, 1), ("az", 3, 1), ("rax2", 5, 0),
    ("rax2", 6, 0), ("ax2", 7, 1), ("rbz", 0, 2, 1), ("bown", 7), ("rax1", 7), ("rbz", 2, 3, 1),
    ("bz", 1, 2, 0), ("rax2", 6, 1), ("rbz", 1, 3, 0), ("ax1", 6), ("ax1", 2), ("lap", 0), ("rbz", 2, 3, 0),
    ("rax3", 4), ("raz", 1), ("rbz", 0, 2, 0), ("rbz", 3, 3, 0), ("bz", 1, 2, 1), ("bz", 2, 2, 1),
    ("ax2", 1, 0), ("rbz", 3, 3, 1), ("ax1", 3), ("az", 4, 0), ("az", 4, 1), ("bown", 1), ("rax1", 1),
    ("bz", 0, 3, 0), ("rax2", 2, 0), ("rbz", 1, 3, 1), ("ax1", 5), ("lap", 1), ("rbz", 2, 4, 1),
    ("rax2", 7, 0), ("bz", 2, 2, 0), ("rbz", 2, 4, 0), ("rax3", 5), ("rax2", 2, 1), ("raz", 2, 1),
    ("rax3", 3), ("raz", 2, 0), ("bz", 1, 3, 1), ("rax3", 6), ("ap", 0), ("rax2", 7, 1), ("bz", 3, 3, 0),
    ("bpart", 0), ("bz", 3, 3, 1), ("bz", 2, 3, 1), ("bz", 0, 3, 1), ("bz", 1, 3, 0), ("rbz", 0, 3, 1),
    ("ax1", 4), ("ax2", 3, 0), ("lap", 3), ("bp", 0), ("rbz", 3, 4, 0), ("bown", 0), ("bz", 2, 3, 0),
    ("rax1", 0), ("ax2", 3, 1), ("rbz", 0, 3, 0), ("rbx1",), ("bp", 2, 0), ("rbz", 3, 4, 1), ("rax2", 1, 1),
    ("ax2", 1, 1), ("rax2", 1, 0), ("raz", 3, 1), ("rax3", 2), ("raz", 3, 0), ("rbz", 1, 4, 1),
    ("bz", 1, 4, 1), ("bp", 1, 0), ("ax2", 5, 1), ("ax2", 7, 0), ("ax2", 5, 0), ("lap", 4), ("bp", 2, 1),
    ("rbz", 1, 4, 0), ("bp", 1, 1), ("bz", 0, 4, 0), ("ax2", 6, 1), ("ax2", 6, 0), ("bz", 2, 4, 1),
    ("ax2", 2, 1), ("bz", 1, 4, 0), ("ax2", 2, 0), ("bz", 3, 4, 0), ("bz", 3, 4, 1), ("bp", 3, 1),
    ("ax2", 4, 1), ("bz", 0, 4, 1), ("ax2", 4, 0), ("rax2", 0, 1), ("rax2", 0, 0), ("bp", 3, 0), ("ap", 3),
    ("rbz", 0, 4, 1), ("bz", 2, 4, 0), ("rbz", 0, 4, 0), ("rbx2", 1), ("rax3", 1), ("rax3", 7), ("raz", 4, 1),
    ("raz", 4, 0), ("ap", 1), ("lap", 5), ("ap", 7), ("ap", 5), ("rbx2", 0), ("ap", 6), ("ap", 2), ("ap", 4),
    ("bp", 4), ("lap", 2), ("lap", 6), ("rax3", 0), ("lap", 7), ("agend",), ("fin", 5), ("fin", 7),
    ("fin", 0), ("fin", 6), ("fin", 3), ("fin", 4), ("fin", 2), ("fin", 1), ("rsend",),
)


def half(way, start, size):
    first = (size // TILE + 1) // 2 * TILE
    return (start, first) if way == 0 else (start + first, size - first)


def split_bf16(matrix):
    high = matrix.astype(jnp.bfloat16)
    low = (matrix - high.astype(np.float64)).astype(jnp.bfloat16)
    return high, low


def stencil_matrices():
    along_y, along_x = np.zeros((32, 32)), np.zeros((8, 8))
    left, right, along_z = np.zeros((8, 8)), np.zeros((8, 8)), np.zeros((LANES, LANES))
    for offset in range(1, 9):
        weight = kinetic_taps[offset - 1]
        along_y += weight * (np.eye(32, k=offset) + np.eye(32, k=-offset))
        along_x += weight * (np.eye(8, k=offset) + np.eye(8, k=-offset))
        left += weight * np.eye(8, k=8 - offset)
        right += weight * np.eye(8, k=offset - 8)
        along_z += weight * (
            np.roll(np.eye(LANES), offset, 1) + np.roll(np.eye(LANES), -offset, 1)
        )
    own = (
        np.kron(along_y, np.eye(8))
        + np.kron(np.eye(32), along_x)
        + 3.0 * center_tap * np.eye(ROWS)
    )
    rows = np.concatenate(
        [own, np.kron(np.eye(32), left), np.kron(np.eye(32), right)], axis=1
    )
    rows_high, rows_low = split_bf16(-0.5 * rows)
    z_high, z_low = split_bf16(-0.5 * along_z)
    halves = [part[:, at:at + LANES] for part in (rows_high, rows_low) for at in range(0, 3 * ROWS, LANES)]
    mixes = np.stack([*halves, np.concatenate([z_high, z_low], axis=0)])
    return mixes.reshape(len(mixes), PLANES, 8, LANES)


def kernel(
    corners_in, occupation_in, support, potential, mixes_in,
    applied, density,
    corners, occupation, weights, own, left, right, pot_in, mixes,
    kinetic, gathered, terms, table, part_out, part_in, sums,
    xa1, xa2, za1, za, zb1, zb, xb1, xb2, tally,
    load_sem, send_sem, recv_sem,
):
    f32, bf16 = jnp.float32, jnp.bfloat16
    group, slab = lax.axis_index("grp"), lax.axis_index("slab")
    x, z, core = group // 16, (group // 2) % 8, group % 2

    def chip(dx, dz):
        return ((((x + dx) % NXC) * NZC + (z + dz) % NZC) * 2 + core, slab)

    partner = (group + 1 - 2 * core, slab)
    x_next, x_prev = chip(1, 0), chip(NXC - 1, 0)
    z_next, z_prev = chip(0, 1), chip(0, NZC - 1)
    y_next, y_prev = (group, (slab + 1) % 4), (group, (slab + 3) % 4)
    along_x, along_z, along_y = (x_next, x_prev), (z_next, z_prev), (y_next, y_prev)

    barrier = pltpu.get_barrier_semaphore()
    neighbours = (*along_x, *along_z, *along_y, partner)
    for device in neighbours:
        pl.semaphore_signal(barrier, inc=1, device_id=device, device_id_type=MESH)

    loads = {}
    for index, (name, src, dst) in enumerate([
        ("corners", corners_in, corners),
        ("potential", potential, pot_in),
        ("occupation", occupation_in, occupation),
        ("support", support, own),
        ("mixes", mixes_in.reshape(mixes.shape), mixes),
    ]):
        loads[name] = pltpu.make_async_copy(src, dst, load_sem.at[index])
        loads[name].start()

    slots, pending, rows = {}, {}, []

    def send(name, src, dst, device):
        index = slots.setdefault(name, len(slots))
        rows.append(math.prod(src.shape[:-1]))
        pending[name] = pending.get(name, 0) + rows[-1]
        pltpu.make_async_remote_copy(
            src_ref=src, dst_ref=dst,
            send_sem=send_sem, recv_sem=recv_sem.at[index],
            device_id=device, device_id_type=MESH,
        ).start()

    def arrived(*name):
        if name in pending:
            whole = tally.at[pl.ds(0, pending.pop(name))]
            pltpu.make_async_copy(whole, whole, recv_sem.at[slots[name]]).wait()

    def slot(dx, dz, start, size):
        tiles = pl.ds(start // TILE, size // TILE)
        return gathered.at[(x + dx) % NXC, (z + dz) % NZC, core, tiles]

    def column(dz, start, size):
        tiles = pl.ds(start // TILE, size // TILE)
        return gathered.at[pl.ds(0, NXC), (z + dz) % NZC, core, tiles]

    def from_way(way, distance):
        return (NZC - distance) % NZC if way == 0 else distance

    def az(step, way):
        if step > 1:
            arrived("az", step - 1, way)
        dz = from_way(way, step - 1)
        where = slot(0, dz, *((0, GA) if step < 4 else half(way, 0, GA)))
        send(("az", 4) if step == 4 else ("az", step, way), where, where, along_z[way])

    def ax1(dz):
        if dz == 4:
            arrived("az", 4)
        elif dz:
            arrived("az", min(dz, NZC - dz), 0 if dz > 4 else 1)
        for way in range(2):
            where = slot(0, dz, 0, GA)
            send(("ax1", dz, way), where, where, along_x[way])

    def ax2(dz, way):
        arrived("ax1", dz, way)
        where = slot(3 if way == 0 else 1, dz, *half(way, 0, GA))
        send(("ax2", dz), where, where, along_x[way])

    def ap(dz):
        arrived("ax2", dz)
        where = column(dz, 0, GA)
        send(("ap",), where, where, partner)

    def bx1():
        for way in range(2):
            where = slot(0, 0, GA, GB)
            send(("bx1", way), where, where, along_x[way])

    def bx2(way):
        arrived("bx1", way)
        where = slot(3 if way == 0 else 1, 0, *half(way, GA, GB))
        send(("bx2",), where, where, along_x[way])

    def bz(dx, step, way):
        if step > 1:
            arrived("bz", dx, step - 1, way)
        elif dx == 2:
            arrived("bx2")
        elif dx:
            arrived("bx1", 0 if dx == 3 else 1)
        dz = from_way(way, step - 1)
        where = slot(dx, dz, *((GA, GB) if step < 4 else half(way, GA, GB)))
        send(("bz", dx, 4) if step == 4 else ("bz", dx, step, way), where, where, along_z[way])

    def bp(distance, way=0):
        if distance == 0:
            arrived("bx1", 0)
            arrived("bx1", 1)
            arrived("bx2")
        elif distance == 4:
            for dx in range(NXC):
                arrived("bz", dx, 4)
        else:
            for dx in range(NXC):
                arrived("bz", dx, distance, way)
        dz = from_way(way, distance)
        where = column(dz, GA, GB)
        send(("ap",), where, where, partner)

    def agend():
        arrived("ap")
        gathered[4, 0, 0] = gathered[0, 0, 0]

    def build(target, dz, owner, added=None):
        shift = corners[0] % PLANES

        def one(dx, carry):
            block = ((x + dx) % NXC) * 16 + ((z + dz) % NZC) * 2 + owner
            after = table[block] - shift
            before = table[(block + 63) % 64] + PLANES - shift
            for at in range(0, PLANES, 2):
                planes = [
                    terms[plane + jnp.where(plane >= shift, after, before)]
                    for plane in (at, at + 1)
                ]
                value = jnp.concatenate(planes, axis=0)
                rows = pl.ds(at * 8, TILE)
                if added is not None:
                    value = value + added[dz, dx, rows, :].astype(f32)
                target[dz, dx, rows, :] = value.astype(bf16)
            return carry

        lax.fori_loop(0, NXC, one, 0)

    def bpart(dz):
        build(part_out, dz, 1 - core)
        send(("part", dz), part_out.at[dz], part_in.at[dz], partner)

    def bown(dz):
        arrived("part", dz)
        build(sums, dz, core, part_in)

    def add(where, start, size, *others):
        total = where[pl.ds(start, size), :].astype(f32)
        for other in others:
            total = total + other[...].astype(f32)
        where[pl.ds(start, size), :] = total.astype(bf16)

    def rax1(dz):
        for way in range(2):
            start, size = half(way, 0, SA)
            part = sums.at[dz, 2, pl.ds(start, size)]
            send(("rax1", dz, way), part, xa1.at[dz, way, pl.ds(0, size)], along_x[way])

    def rax2(dz, way):
        dx = 1 if way == 0 else 3
        arrived("rax1", dz, way)
        start, size = half(way, 0, SA)
        add(sums.at[dz, dx], start, size, xa1.at[dz, way, pl.ds(0, size)])
        part = sums.at[dz, dx, pl.ds(0, SA)]
        send(("rax2", dz), part, xa2.at[dz, way], along_x[way])

    def rax3(dz):
        arrived("rax2", dz)
        add(sums.at[dz, 0], 0, SA, xa2.at[dz, 0], xa2.at[dz, 1])

    def raz(step, way=None):
        if step == 1:
            for way in range(2):
                start, size = half(way, 0, SA)
                part = sums.at[4, 0, pl.ds(start, size)]
                send(("raz", 1, way), part, za1.at[way, pl.ds(0, size)], along_z[way])
            return
        dz = 5 - step if way == 0 else 3 + step
        arrived("raz", step - 1, way)
        if step == 2:
            start, size = half(way, 0, SA)
            add(sums.at[dz, 0], start, size, za1.at[way, pl.ds(0, size)])
        else:
            add(sums.at[dz, 0], 0, SA, za.at[step - 3, way])
        part = sums.at[dz, 0, pl.ds(0, SA)]
        send(("raz", 4) if step == 4 else ("raz", step, way), part, za.at[step - 2, way], along_z[way])

    def rbz(dx, step, way=None):
        if step == 1:
            for way in range(2):
                start, size = half(way, SA, SB)
                part = sums.at[4, dx, pl.ds(start, size)]
                send(("rbz", dx, 1, way), part, zb1.at[way, dx, pl.ds(0, size)], along_z[way])
            return
        dz = 5 - step if way == 0 else 3 + step
        arrived("rbz", dx, step - 1, way)
        if step == 2:
            start, size = half(way, SA, SB)
            add(sums.at[dz, dx], start, size, zb1.at[way, dx, pl.ds(0, size)])
        else:
            add(sums.at[dz, dx], SA, SB, zb.at[step - 3, way, dx])
        part = sums.at[dz, dx, pl.ds(SA, SB)]
        send(("rbz", dx, 4) if step == 4 else ("rbz", dx, step, way), part, zb.at[step - 2, way, dx], along_z[way])

    def rbz_end(dx):
        arrived("rbz", dx, 4)
        add(sums.at[0, dx], SA, SB, zb.at[2, 0, dx], zb.at[2, 1, dx])

    def rbx1():
        rbz_end(2)
        for way in range(2):
            start, size = half(way, SA, SB)
            part = sums.at[0, 2, pl.ds(start, size)]
            send(("rbx1", way), part, xb1.at[way, pl.ds(0, size)], along_x[way])

    def rbx2(way):
        dx = 1 if way == 0 else 3
        rbz_end(dx)
        arrived("rbx1", way)
        start, size = half(way, SA, SB)
        add(sums.at[0, dx], start, size, xb1.at[way, pl.ds(0, size)])
        send(("rbx2",), sums.at[0, dx, pl.ds(SA, SB)], xb2.at[way], along_x[way])

    def rsend():
        arrived("raz", 4)
        arrived("rbz", 0, 4)
        arrived("rbx2")
        density[pl.ds(0, SA), :] = (
            sums[0, 0, pl.ds(0, SA), :].astype(f32)
            + za[2, 0].astype(f32) + za[2, 1].astype(f32)
        )
        density[pl.ds(SA, SB), :] = (
            sums[0, 0, pl.ds(SA, SB), :].astype(f32)
            + zb[2, 0, 0].astype(f32) + zb[2, 1, 0].astype(f32)
            + xb2[0].astype(f32) + xb2[1].astype(f32)
        )

    def halo():
        for pair in range(PAIRS):
            where = pl.ds(2 * pair, 2)
            send(("halo", pair), support.at[where], left.at[where], y_next)
            send(("halo", pair), support.at[where], right.at[where], y_prev)

    def lap(pair):
        if pair == first_lap:
            loads["mixes"].wait()
        arrived("halo", pair)
        first = 2 * pair
        cells = jnp.concatenate([
            jnp.concatenate([ref[first], ref[first + 1]], axis=1) for ref in (own, left, right)
        ], axis=0)
        high, low = (
            jnp.concatenate([mixes[at + piece] for piece in range(6)], axis=1) for at in (0, 6)
        )
        total = jnp.dot(high, cells, preferred_element_type=f32)
        total = total + jnp.dot(low, cells, preferred_element_type=f32)
        for index in range(2):
            values = own[first + index]
            twice = jnp.concatenate([values, values], axis=1)
            kinetic[first + index] = total[:, index * LANES:(index + 1) * LANES] + jnp.dot(
                twice, mixes[12], preferred_element_type=f32
            )

    def fin(pair):
        first = 2 * pair
        flat = gathered.reshape(5 * NZC * 2 * TILES, TILE, LANES)
        for func in (first, first + 1):
            corner = corners[func]
            window = flat[pl.ds(corner // 2, TILES + 1)].astype(f32).reshape(ROWS + TILE, LANES)
            local = jnp.where(corner % 2 == 1, window[8:8 + ROWS], window[:ROWS])
            term = (local * own[func].astype(f32)).astype(bf16).astype(f32)
            applied[func] = (kinetic[func] + term).astype(bf16)

    loads["corners"].wait()
    bases = [corners[k] // 32 for k in range(FUNCS)]

    def find(block, carry):
        found = FUNCS
        for k in reversed(range(FUNCS)):
            found = jnp.where(bases[k] == block, k, found)
        table[block] = found * PLANES
        return carry

    lax.fori_loop(0, 64, find, 0)
    terms[pl.ds(FUNCS * PLANES, PLANES)] = jnp.zeros((PLANES, 8, LANES), f32)
    loads["potential"].wait()
    gathered[x, z, core] = pot_in[...].astype(bf16).reshape(TILES, TILE, LANES)
    loads["occupation"].wait()
    loads["support"].wait()
    spread = jnp.broadcast_to(occupation[...].astype(f32).reshape(1, FUNCS), (FUNCS, FUNCS))
    lane = lax.broadcasted_iota(jnp.int32, (FUNCS, FUNCS), 1)
    diagonal = lane == lax.broadcasted_iota(jnp.int32, (FUNCS, FUNCS), 0)
    column_weights = jnp.sum(jnp.where(diagonal, spread, 0.0), axis=1, keepdims=True)
    for k in range(FUNCS):
        weights[k] = jnp.broadcast_to(column_weights[k:k + 1], (8, LANES))
    weights[FUNCS] = jnp.zeros((8, LANES), f32)

    for k in range(FUNCS):
        value = own[k].astype(f32).reshape(PLANES, 8, LANES)
        total = weights[k] * value * value
        if k + 1 < FUNCS:
            twin = FUNCS
            for other in reversed(range(k + 1, FUNCS)):
                twin = jnp.where(bases[other] == bases[k], other, twin)
            second = own[jnp.minimum(twin, FUNCS - 1)].astype(f32).reshape(PLANES, 8, LANES)
            total = total + weights[twin] * second * second
        terms[pl.ds(k * PLANES, PLANES)] = total
    pl.semaphore_wait(barrier, len(neighbours))

    steps = {step.__name__: step for step in (
        az, ax1, ax2, ap, bx1, bx2, bz, bp, agend, bpart, bown, rax1, rax2, rax3,
        raz, rbz, rbx1, rbx2, rsend, halo, lap, fin,
    )}
    first_lap = next(args[0] for name, *args in ORDER if name == "lap")
    for name, *args in ORDER:
        steps[name](*args)
    assert sum(rows) == SENT_ROWS, sum(rows)
    pltpu.make_async_copy(tally, tally, send_sem).wait()


def store(applied, density, applied_out, density_out, sems):
    copies = [
        pltpu.make_async_copy(applied, applied_out, sems.at[0]),
        pltpu.make_async_copy(density, density_out, sems.at[1]),
    ]
    for copy in copies:
        copy.start()
    for copy in copies:
        copy.wait()


def on_device(support, corners, occupation, potential):
    mixes = stencil_matrices()
    bf16, f32 = jnp.bfloat16, jnp.float32
    vmem = lambda shape, kind=bf16: pltpu.VMEM(shape, kind)
    in_hbm = lambda array: pltpu.with_memory_space_constraint(array, pltpu.HBM)
    anywhere = pl.BlockSpec(memory_space=pl.ANY)
    in_vmem = pl.BlockSpec(memory_space=pltpu.VMEM)
    copies = 144
    applied, density = pl.pallas_call(
        kernel,
        out_shape=(
            pltpu.VMEM((FUNCS, ROWS, LANES), bf16),
            pltpu.VMEM((ROWS, LANES), f32),
        ),
        in_specs=[anywhere] * 5,
        out_specs=(in_vmem, in_vmem),
        scratch_shapes=[
            pltpu.SMEM((FUNCS,), jnp.int32),
            vmem((FUNCS,)),
            vmem((FUNCS + 1, 8, LANES), f32),
            vmem((FUNCS, ROWS, LANES)),
            vmem((FUNCS, ROWS, LANES)),
            vmem((FUNCS, ROWS, LANES)),
            vmem((ROWS, LANES), f32),
            vmem((len(mixes), ROWS, LANES)),
            vmem((FUNCS, ROWS, LANES), f32),
            vmem((NXC + 1, NZC, 2, TILES, TILE, LANES)),
            vmem(((FUNCS + 1) * PLANES, 8, LANES), f32),
            pltpu.SMEM((64,), jnp.int32),
            vmem((NZC, NXC, ROWS, LANES)),
            vmem((NZC, NXC, ROWS, LANES)),
            vmem((NZC, NXC, ROWS, LANES)),
            vmem((NZC, 2, half(0, 0, SA)[1], LANES)),
            vmem((NZC, 2, SA, LANES)),
            vmem((2, half(0, 0, SA)[1], LANES)),
            vmem((3, 2, SA, LANES)),
            vmem((2, NXC, half(0, 0, SB)[1], LANES)),
            vmem((3, 2, NXC, SB, LANES)),
            vmem((2, half(0, 0, SB)[1], LANES)),
            vmem((2, SB, LANES)),
            vmem((SENT_ROWS, LANES)),
            pltpu.SemaphoreType.DMA((5,)),
            pltpu.SemaphoreType.DMA,
            pltpu.SemaphoreType.DMA((copies,)),
        ],
        compiler_params=pltpu.CompilerParams(
            collective_id=0, has_side_effects=True, vmem_limit_bytes=48 * 1024 * 1024
        ),
    )(
        in_hbm(corners),
        in_hbm(occupation),
        in_hbm(support.reshape(FUNCS, ROWS, LANES)),
        in_hbm(potential.reshape(ROWS, LANES)),
        in_hbm(jnp.asarray(mixes)),
    )
    applied, density = pl.pallas_call(
        store,
        out_shape=(
            jax.ShapeDtypeStruct((FUNCS, ROWS, LANES), bf16),
            jax.ShapeDtypeStruct((ROWS, LANES), f32),
        ),
        in_specs=[anywhere] * 2,
        out_specs=(anywhere, anywhere),
        scratch_shapes=[pltpu.SemaphoreType.DMA((2,))],
        compiler_params=pltpu.CompilerParams(vmem_limit_bytes=8 * 1024 * 1024),
    )(applied, density)
    return applied.reshape(support.shape), density.reshape(potential.shape)


def solution(mesh):
    in_specs = (P("grp", None, "slab", None), P("grp"), P("grp"), P("grp", "slab", None))
    out_specs = (P("grp", None, "slab", None), P("grp", "slab", None))
    return jax.shard_map(
        on_device, mesh=mesh, in_specs=in_specs, out_specs=out_specs, check_vma=False
    )
```

```python
import functools
import math

import jax
import jax.numpy as jnp
import numpy as np
from jax import lax
from jax.experimental import pallas as pl
from jax.experimental.pallas import tpu as pltpu
from jax.sharding import PartitionSpec as P

MESH = pl.DeviceIdType.MESH
FUNCS, ROWS, LANES = 16, 256, 128
NXC, NZC = 4, 8
PAIRS = FUNCS // 2
TILE = 16
PLANES, TILES = ROWS // 8, ROWS // TILE
RA = 160
RB = ROWS - RA
HA, HB = RA // 2, RB // 2
EARLY = (4, 5, 3,)
STORES = 4
SENT_ROWS = 40448

kinetic_taps = [
    2.0 * (-1.0) ** (index + 2) / float((index + 1) * (index + 1)) for index in range(8)
]
center_tap = -math.pi * math.pi / 3.0


ORDER = (
    ("az", 1, 1), ("bx1",), ("az", 1, 0), ("bpart", 4), ("ax1", 0), ("bpart", 5), ("halo",), ("bpart", 3),
    ("bown", 4), ("rax1", 4), ("rbz", 1, 1), ("bown", 5), ("rax1", 5), ("rbz", 2, 1), ("bx2", 0), ("bx2", 1),
    ("ax1", 1), ("az", 2, 0), ("az", 2, 1), ("bown", 3), ("rax1", 3), ("rbz", 0, 1), ("bpart", 6), ("ax1", 7),
    ("ax2", 0, 1), ("bpart", 2), ("rbz", 3, 1), ("rbz", 1, 2, 0), ("rbz", 1, 2, 1), ("rax2", 4, 0),
    ("rax2", 4, 1), ("rbz", 2, 2, 1), ("rbz", 2, 2, 0), ("bz", 1, 1), ("bz", 1, 0), ("ax2", 0, 0),
    ("bown", 2), ("rax1", 2), ("bown", 6), ("rax1", 6), ("rax2", 5, 1), ("az", 3, 0), ("rax2", 5, 0),
    ("bpart", 7), ("rbz", 3, 2, 0), ("rbz", 3, 2, 1), ("rax2", 3, 1), ("rax2", 3, 0), ("az", 3, 1),
    ("ax1", 6), ("rbz", 2, 3, 0), ("ax1", 2), ("rbz", 0, 2, 1), ("rax3", 4), ("raz", 1), ("bown", 7),
    ("bpart", 1), ("rbz", 2, 3, 1), ("rbz", 0, 2, 0), ("rax2", 6, 1), ("rax1", 7), ("rax2", 6, 0),
    ("rax2", 2, 0), ("bz", 2, 1), ("bz", 2, 0), ("rbz", 1, 3, 1), ("rax3", 5), ("bpart", 0), ("ax2", 1, 1),
    ("ax2", 7, 1), ("az", 4, 0), ("ax2", 1, 0), ("az", 4, 1), ("bown", 1), ("rax2", 2, 1), ("rbz", 1, 3, 0),
    ("rbz", 3, 3, 1), ("bown", 0), ("rax1", 0), ("rax1", 1), ("rbz", 2, 4, 0), ("rbz", 3, 3, 0),
    ("rbz", 2, 4, 1), ("ax2", 7, 0), ("ap", 0), ("raz", 2, 1), ("ax2", 6, 1), ("ax2", 2, 1), ("ax1", 5),
    ("ax2", 2, 0), ("rax3", 3), ("raz", 2, 0), ("ax1", 3), ("bz", 3, 1), ("bz", 3, 0), ("rax3", 6),
    ("bp", 1, 1), ("lap", 2), ("ax1", 4), ("bp", 2, 1), ("rax2", 7, 1), ("ax2", 6, 0), ("lap", 0),
    ("rbz", 0, 3, 1), ("rax2", 1, 1), ("rbz", 0, 3, 0), ("rbz", 3, 4, 1), ("rax2", 7, 0), ("lap", 3),
    ("rbz", 1, 4, 0), ("ap", 1), ("raz", 3, 1), ("rax2", 1, 0), ("rax3", 2), ("raz", 3, 0), ("rbx1",),
    ("rbz", 3, 4, 0), ("ax2", 5, 1), ("rbz", 1, 4, 1), ("ax2", 5, 0), ("ax2", 3, 0), ("ap", 7), ("ax2", 3, 1),
    ("bz", 4, 1), ("bz", 4, 0), ("ax2", 4, 0), ("bp", 1, 0), ("ax2", 4, 1), ("rax2", 0, 1), ("rax2", 0, 0),
    ("bp", 0), ("rbz", 0, 4, 1), ("lap", 5), ("bp", 3, 0), ("rbz", 0, 4, 0), ("ap", 2), ("ap", 6),
    ("rax3", 7), ("bp", 3, 1), ("bp", 2, 0), ("raz", 4, 1), ("rax3", 1), ("raz", 4, 0), ("rbx2", 0),
    ("rbx2", 1), ("ap", 5), ("ap", 3), ("lap", 1), ("ap", 4), ("bp", 4), ("lap", 4), ("lap", 6), ("rax3", 0),
    ("lap", 7), ("agend",), ("fin", 1), ("fin", 5), ("fin", 0), ("fin", 4), ("fin", 3), ("fin", 2),
    ("fin", 6), ("fin", 7), ("rsend",),
)


def split_bf16(matrix):
    high = matrix.astype(jnp.bfloat16)
    low = (matrix - high.astype(np.float64)).astype(jnp.bfloat16)
    return high, low


def stencil_matrices():
    along_y, along_x = np.zeros((32, 32)), np.zeros((8, 8))
    left, right, along_z = np.zeros((8, 8)), np.zeros((8, 8)), np.zeros((LANES, LANES))
    for offset in range(1, 9):
        weight = kinetic_taps[offset - 1]
        along_y += weight * (np.eye(32, k=offset) + np.eye(32, k=-offset))
        along_x += weight * (np.eye(8, k=offset) + np.eye(8, k=-offset))
        left += weight * np.eye(8, k=8 - offset)
        right += weight * np.eye(8, k=offset - 8)
        along_z += weight * (
            np.roll(np.eye(LANES), offset, 1) + np.roll(np.eye(LANES), -offset, 1)
        )
    own = (
        np.kron(along_y, np.eye(8))
        + np.kron(np.eye(32), along_x)
        + 3.0 * center_tap * np.eye(ROWS)
    )
    rows = np.concatenate(
        [own, np.kron(np.eye(32), left), np.kron(np.eye(32), right)], axis=1
    )
    rows_high, rows_low = split_bf16(-0.5 * rows)
    z_high, z_low = split_bf16(-0.5 * along_z)
    halves = [part[:, at:at + LANES] for part in (rows_high, rows_low) for at in range(0, 3 * ROWS, LANES)]
    mixes = np.stack([*halves, np.concatenate([z_high, z_low], axis=0)])
    return mixes.reshape(len(mixes), PLANES, 8, LANES)


def kernel(
    corners_in, occupation_in, support, potential, mixes_in,
    applied, density,
    corners, occupation, weights, own, left, right, pot_in, mixes,
    kinetic, gathered, terms, table, part_out, part_in, sums,
    xa1, xa2, za1, za, zb1, zb, xb1, xb2, tally,
    load_sem, send_sem, recv_sem,
):
    f32, bf16 = jnp.float32, jnp.bfloat16
    group, slab = lax.axis_index("grp"), lax.axis_index("slab")
    x, z, core = group // 16, (group // 2) % 8, group % 2

    def chip(dx, dz):
        return ((((x + dx) % NXC) * NZC + (z + dz) % NZC) * 2 + core, slab)

    partner = (group + 1 - 2 * core, slab)
    x_next, x_prev = chip(1, 0), chip(NXC - 1, 0)
    z_next, z_prev = chip(0, 1), chip(0, NZC - 1)
    y_next, y_prev = (group, (slab + 1) % 4), (group, (slab + 3) % 4)
    along_x, along_z, along_y = (x_next, x_prev), (z_next, z_prev), (y_next, y_prev)

    barrier = pltpu.get_barrier_semaphore()
    neighbours = (*along_x, *along_z, *along_y, partner)
    for device in neighbours:
        pl.semaphore_signal(barrier, inc=1, device_id=device, device_id_type=MESH)

    loads = {}
    for index, (name, src, dst) in enumerate([
        ("corners", corners_in, corners),
        ("potential", potential, pot_in),
        ("occupation", occupation_in, occupation),
        ("support", support, own),
        ("mixes", mixes_in.reshape(mixes.shape), mixes),
    ]):
        loads[name] = pltpu.make_async_copy(src, dst, load_sem.at[index])
        loads[name].start()

    slots, pending, rows = {}, {}, []

    def send(name, src, dst, device):
        index = slots.setdefault(name, len(slots))
        rows.append(math.prod(src.shape[:-1]))
        pending[name] = pending.get(name, 0) + rows[-1]
        pltpu.make_async_remote_copy(
            src_ref=src, dst_ref=dst,
            send_sem=send_sem, recv_sem=recv_sem.at[index],
            device_id=device, device_id_type=MESH,
        ).start()

    def arrived(*name):
        if name in pending:
            whole = tally.at[pl.ds(0, pending.pop(name))]
            pltpu.make_async_copy(whole, whole, recv_sem.at[slots[name]]).wait()

    def slot(dx, dz, start, size):
        tiles = pl.ds(start // TILE, size // TILE)
        return gathered.at[(x + dx) % NXC, (z + dz) % NZC, core, tiles]

    def column(dz, start, size):
        tiles = pl.ds(start // TILE, size // TILE)
        return gathered.at[pl.ds(0, NXC), (z + dz) % NZC, core, tiles]

    def from_way(way, distance):
        return (NZC - distance) % NZC if way == 0 else distance

    def az(step, way):
        if step > 1:
            arrived("az", step - 1, way)
        dz = from_way(way, step - 1)
        where = slot(0, dz, 0, RA) if step < 4 else slot(0, dz, way * HA, HA)
        send(("az", 4) if step == 4 else ("az", step, way), where, where, along_z[way])

    def ax1(dz):
        if dz == 4:
            arrived("az", 4)
        elif dz:
            arrived("az", min(dz, NZC - dz), 0 if dz > 4 else 1)
        for way in range(2):
            where = slot(0, dz, 0, RA)
            send(("ax1", dz, way), where, where, along_x[way])

    def ax2(dz, way):
        arrived("ax1", dz, way)
        where = slot(3 if way == 0 else 1, dz, way * HA, HA)
        send(("ax2", dz), where, where, along_x[way])

    def ap(dz):
        arrived("ax2", dz)
        where = column(dz, 0, RA)
        send(("ap",), where, where, partner)

    def bx1():
        for way in range(2):
            where = slot(0, 0, RA, RB)
            send(("bx1", way), where, where, along_x[way])

    def bx2(way):
        arrived("bx1", way)
        where = slot(3 if way == 0 else 1, 0, RA + way * HB, HB)
        send(("bx2",), where, where, along_x[way])

    def bz(step, way):
        if step == 1:
            arrived("bx2")
        else:
            arrived("bz", step - 1, way)
        dz = from_way(way, step - 1)
        where = column(dz, RA, RB) if step < 4 else column(dz, RA + way * HB, HB)
        send(("bz", 4) if step == 4 else ("bz", step, way), where, where, along_z[way])

    def bp(distance, way=0):
        if distance == 0:
            arrived("bx2")
        elif distance == 4:
            arrived("bz", 4)
        else:
            arrived("bz", distance, way)
        dz = from_way(way, distance)
        where = column(dz, RA, RB)
        send(("ap",), where, where, partner)

    def agend():
        arrived("ap")
        gathered[4, 0, 0] = gathered[0, 0, 0]

    def build(target, dz, owner, added=None):
        shift = corners[0] % PLANES

        def one(dx, carry):
            block = ((x + dx) % NXC) * 16 + ((z + dz) % NZC) * 2 + owner
            after = table[block] - shift
            before = table[(block + 63) % 64] + PLANES - shift
            for at in range(0, PLANES, 2):
                planes = [
                    terms[plane + jnp.where(plane >= shift, after, before)]
                    for plane in (at, at + 1)
                ]
                value = jnp.concatenate(planes, axis=0)
                rows = pl.ds(at * 8, TILE)
                if added is not None:
                    value = value + added[dz, dx, rows, :].astype(f32)
                target[dz, dx, rows, :] = value.astype(bf16)
            return carry

        lax.fori_loop(0, NXC, one, 0)

    def bpart(dz):
        if dz not in EARLY:
            build(part_out, dz, 1 - core)
        send(("part", dz), part_out.at[dz], part_in.at[dz], partner)

    def bown(dz):
        arrived("part", dz)
        build(sums, dz, core, part_in)

    def add(where, start, size, *others):
        total = where[pl.ds(start, size), :].astype(f32)
        for other in others:
            total = total + other[...].astype(f32)
        where[pl.ds(start, size), :] = total.astype(bf16)

    def rax1(dz):
        for way in range(2):
            part = sums.at[dz, 2, pl.ds(way * HA, HA)]
            send(("rax1", dz, way), part, xa1.at[dz, way], along_x[way])

    def rax2(dz, way):
        dx = 1 if way == 0 else 3
        arrived("rax1", dz, way)
        add(sums.at[dz, dx], way * HA, HA, xa1.at[dz, way])
        part = sums.at[dz, dx, pl.ds(0, RA)]
        send(("rax2", dz), part, xa2.at[dz, way], along_x[way])

    def rax3(dz):
        arrived("rax2", dz)
        add(sums.at[dz, 0], 0, RA, xa2.at[dz, 0], xa2.at[dz, 1])

    def raz(step, way=None):
        if step == 1:
            for way in range(2):
                part = sums.at[4, 0, pl.ds(way * HA, HA)]
                send(("raz", 1, way), part, za1.at[way], along_z[way])
            return
        dz = 5 - step if way == 0 else 3 + step
        arrived("raz", step - 1, way)
        if step == 2:
            add(sums.at[dz, 0], way * HA, HA, za1.at[way])
        else:
            add(sums.at[dz, 0], 0, RA, za.at[step - 3, way])
        part = sums.at[dz, 0, pl.ds(0, RA)]
        send(("raz", 4) if step == 4 else ("raz", step, way), part, za.at[step - 2, way], along_z[way])

    def rbz(dx, step, way=None):
        if step == 1:
            for way in range(2):
                part = sums.at[4, dx, pl.ds(RA + way * HB, HB)]
                send(("rbz", dx, 1, way), part, zb1.at[way, dx], along_z[way])
            return
        dz = 5 - step if way == 0 else 3 + step
        arrived("rbz", dx, step - 1, way)
        if step == 2:
            add(sums.at[dz, dx], RA + way * HB, HB, zb1.at[way, dx])
        else:
            add(sums.at[dz, dx], RA, RB, zb.at[step - 3, way, dx])
        part = sums.at[dz, dx, pl.ds(RA, RB)]
        send(("rbz", dx, 4) if step == 4 else ("rbz", dx, step, way), part, zb.at[step - 2, way, dx], along_z[way])

    def rbz_end(dx):
        arrived("rbz", dx, 4)
        add(sums.at[0, dx], RA, RB, zb.at[2, 0, dx], zb.at[2, 1, dx])

    def rbx1():
        rbz_end(2)
        for way in range(2):
            part = sums.at[0, 2, pl.ds(RA + way * HB, HB)]
            send(("rbx1", way), part, xb1.at[way], along_x[way])

    def rbx2(way):
        dx = 1 if way == 0 else 3
        rbz_end(dx)
        arrived("rbx1", way)
        add(sums.at[0, dx], RA + way * HB, HB, xb1.at[way])
        send(("rbx2",), sums.at[0, dx, pl.ds(RA, RB)], xb2.at[way], along_x[way])

    def rsend():
        arrived("raz", 4)
        arrived("rbz", 0, 4)
        arrived("rbx2")
        density[pl.ds(0, RA), :] = (
            sums[0, 0, pl.ds(0, RA), :].astype(f32)
            + za[2, 0].astype(f32) + za[2, 1].astype(f32)
        )
        density[pl.ds(RA, RB), :] = (
            sums[0, 0, pl.ds(RA, RB), :].astype(f32)
            + zb[2, 0, 0].astype(f32) + zb[2, 1, 0].astype(f32)
            + xb2[0].astype(f32) + xb2[1].astype(f32)
        )

    def halo():
        for pair in range(PAIRS):
            where = pl.ds(2 * pair, 2)
            send(("halo", pair), support.at[where], left.at[where], y_next)
            send(("halo", pair), support.at[where], right.at[where], y_prev)

    def lap(pair):
        if pair == first_lap:
            loads["mixes"].wait()
        arrived("halo", pair)
        first = 2 * pair
        cells = jnp.concatenate([
            jnp.concatenate([ref[first], ref[first + 1]], axis=1) for ref in (own, left, right)
        ], axis=0)
        high, low = (
            jnp.concatenate([mixes[at + piece] for piece in range(6)], axis=1) for at in (0, 6)
        )
        total = jnp.dot(high, cells, preferred_element_type=f32)
        total = total + jnp.dot(low, cells, preferred_element_type=f32)
        for index in range(2):
            values = own[first + index]
            twice = jnp.concatenate([values, values], axis=1)
            kinetic[first + index] = total[:, index * LANES:(index + 1) * LANES] + jnp.dot(
                twice, mixes[12], preferred_element_type=f32
            )

    def fin(pair):
        first = 2 * pair
        flat = gathered.reshape(5 * NZC * 2 * TILES, TILE, LANES)
        for func in (first, first + 1):
            corner = corners[func]
            window = flat[pl.ds(corner // 2, TILES + 1)].astype(f32).reshape(ROWS + TILE, LANES)
            local = jnp.where(corner % 2 == 1, window[8:8 + ROWS], window[:ROWS])
            term = (local * own[func].astype(f32)).astype(bf16).astype(f32)
            applied[func] = (kinetic[func] + term).astype(bf16)

    loads["corners"].wait()
    bases = [corners[k] // 32 for k in range(FUNCS)]

    def find(block, carry):
        found = FUNCS
        for k in reversed(range(FUNCS)):
            found = jnp.where(bases[k] == block, k, found)
        table[block] = found * PLANES
        return carry

    lax.fori_loop(0, 64, find, 0)
    terms[pl.ds(FUNCS * PLANES, PLANES)] = jnp.zeros((PLANES, 8, LANES), f32)
    loads["potential"].wait()
    gathered[x, z, core] = pot_in[...].astype(bf16).reshape(TILES, TILE, LANES)
    loads["occupation"].wait()
    loads["support"].wait()
    spread = jnp.broadcast_to(occupation[...].astype(f32).reshape(1, FUNCS), (FUNCS, FUNCS))
    lane = lax.broadcasted_iota(jnp.int32, (FUNCS, FUNCS), 1)
    diagonal = lane == lax.broadcasted_iota(jnp.int32, (FUNCS, FUNCS), 0)
    column_weights = jnp.sum(jnp.where(diagonal, spread, 0.0), axis=1, keepdims=True)
    for k in range(FUNCS):
        weights[k] = jnp.broadcast_to(column_weights[k:k + 1], (8, LANES))
    weights[FUNCS] = jnp.zeros((8, LANES), f32)

    for k in range(FUNCS):
        value = own[k].astype(f32).reshape(PLANES, 8, LANES)
        total = weights[k] * value * value
        if k + 1 < FUNCS:
            twin = FUNCS
            for other in reversed(range(k + 1, FUNCS)):
                twin = jnp.where(bases[other] == bases[k], other, twin)
            second = own[jnp.minimum(twin, FUNCS - 1)].astype(f32).reshape(PLANES, 8, LANES)
            total = total + weights[twin] * second * second
        terms[pl.ds(k * PLANES, PLANES)] = total
    for dz in EARLY:
        build(part_out, dz, 1 - core)
    pl.semaphore_wait(barrier, len(neighbours))

    steps = {step.__name__: step for step in (
        az, ax1, ax2, ap, bx1, bx2, bz, bp, agend, bpart, bown, rax1, rax2, rax3,
        raz, rbz, rbx1, rbx2, rsend, halo, lap, fin,
    )}
    first_lap = next(args[0] for name, *args in ORDER if name == "lap")
    for name, *args in ORDER:
        steps[name](*args)
    assert sum(rows) == SENT_ROWS, sum(rows)
    pltpu.make_async_copy(tally, tally, send_sem).wait()


def store(applied, density, applied_out, density_out, sems):
    copies = [pltpu.make_async_copy(density, density_out, sems.at[STORES])]
    for piece in range(STORES):
        where = pl.ds(piece * FUNCS // STORES, FUNCS // STORES)
        copies.append(
            pltpu.make_async_copy(applied.at[where], applied_out.at[where], sems.at[piece])
        )
    for copy in copies:
        copy.start()
    for copy in copies:
        copy.wait()


def on_device(support, corners, occupation, potential):
    mixes = stencil_matrices()
    bf16, f32 = jnp.bfloat16, jnp.float32
    vmem = lambda shape, kind=bf16: pltpu.VMEM(shape, kind)
    in_hbm = lambda array: pltpu.with_memory_space_constraint(array, pltpu.HBM)
    anywhere = pl.BlockSpec(memory_space=pl.ANY)
    in_vmem = pl.BlockSpec(memory_space=pltpu.VMEM)
    copies = 122
    applied, density = pl.pallas_call(
        kernel,
        out_shape=(
            pltpu.VMEM((FUNCS, ROWS, LANES), bf16),
            pltpu.VMEM((ROWS, LANES), f32),
        ),
        in_specs=[anywhere] * 5,
        out_specs=(in_vmem, in_vmem),
        scratch_shapes=[
            pltpu.SMEM((FUNCS,), jnp.int32),
            vmem((FUNCS,)),
            vmem((FUNCS + 1, 8, LANES), f32),
            vmem((FUNCS, ROWS, LANES)),
            vmem((FUNCS, ROWS, LANES)),
            vmem((FUNCS, ROWS, LANES)),
            vmem((ROWS, LANES), f32),
            vmem((len(mixes), ROWS, LANES)),
            vmem((FUNCS, ROWS, LANES), f32),
            vmem((NXC + 1, NZC, 2, TILES, TILE, LANES)),
            vmem(((FUNCS + 1) * PLANES, 8, LANES), f32),
            pltpu.SMEM((64,), jnp.int32),
            vmem((NZC, NXC, ROWS, LANES)),
            vmem((NZC, NXC, ROWS, LANES)),
            vmem((NZC, NXC, ROWS, LANES)),
            vmem((NZC, 2, HA, LANES)),
            vmem((NZC, 2, RA, LANES)),
            vmem((2, HA, LANES)),
            vmem((3, 2, RA, LANES)),
            vmem((2, NXC, HB, LANES)),
            vmem((3, 2, NXC, RB, LANES)),
            vmem((2, HB, LANES)),
            vmem((2, RB, LANES)),
            vmem((SENT_ROWS, LANES)),
            pltpu.SemaphoreType.DMA((5,)),
            pltpu.SemaphoreType.DMA,
            pltpu.SemaphoreType.DMA((copies,)),
        ],
        compiler_params=pltpu.CompilerParams(
            collective_id=0, has_side_effects=True, vmem_limit_bytes=48 * 1024 * 1024
        ),
    )(
        in_hbm(corners),
        in_hbm(occupation),
        in_hbm(support.reshape(FUNCS, ROWS, LANES)),
        in_hbm(potential.reshape(ROWS, LANES)),
        in_hbm(jnp.asarray(mixes)),
    )
    applied, density = pl.pallas_call(
        store,
        out_shape=(
            jax.ShapeDtypeStruct((FUNCS, ROWS, LANES), bf16),
            jax.ShapeDtypeStruct((ROWS, LANES), f32),
        ),
        in_specs=[anywhere] * 2,
        out_specs=(anywhere, anywhere),
        scratch_shapes=[pltpu.SemaphoreType.DMA((STORES + 1,))],
        compiler_params=pltpu.CompilerParams(vmem_limit_bytes=8 * 1024 * 1024),
    )(applied, density)
    return applied.reshape(support.shape), density.reshape(potential.shape)


def solution(mesh):
    in_specs = (P("grp", None, "slab", None), P("grp"), P("grp"), P("grp", "slab", None))
    out_specs = (P("grp", None, "slab", None), P("grp", "slab", None))
    return jax.shard_map(
        on_device, mesh=mesh, in_specs=in_specs, out_specs=out_specs, check_vma=False
    )
```
